256 devices in a mesh: row: 8 (over y, x_hi), res: 32 (over x_lo, z, core).
Axes of the slice: x: 4 (x_hi: 2, x_lo: 2; x = x_hi * 2 + x_lo), y: 4, z: 8, core: 2. Of those that a mesh axis runs over, the one named last changes fastest.
Arguments:
- sequence_stack: bfloat16 [256, 2048, 64], P('row', 'res'), may hold values from -40 to 40
- twofold_features: bfloat16 [2048, 2048, 128], P('row', 'res'), may hold values from -40 to 40
- incoming_adjoint: bfloat16 [256, 2048, 64], P('row', 'res'), may hold values from -6 to 6
- sequence_present_flags: int32 [256], P('row'), may hold values 0 or 1
- polymer_identifiers: int32 [2048], replicated, may hold values from 0 to 3, as said below
- sequence_position_ids: int32 [2048], replicated, may hold values from 1 to 41159, as said below
- sequence_stack_multiplier: float32 [64], replicated, may hold values from 0.25 to 1.75
- twofold_stack_multiplier: float32 [128], replicated, may hold values from 0.25 to 1.75
- content_projection: bfloat16 [64, 64], replicated, may hold values from -0.75 to 0.75
- sigmoid_projection: bfloat16 [64, 64], replicated, may hold values from -0.75 to 0.75
- final_projection: bfloat16 [64, 64], replicated, may hold values from -0.75 to 0.75
- twofold_head_projection: float32 [128, 8], replicated, may hold values from -0.5 to 0.5
- separation_bucket_shift: float32 [66, 8], replicated, may hold values from -4 to 450
Outputs:
- alignment_gradient: bfloat16 [256, 2048, 64], P('row', 'res')
- pair_gradient: bfloat16 [2048, 2048, 128], P('row', 'res')
The draws below stay inside these ranges and needn't reach their ends.
Inputs may be any that keep to these rules, and one draw needn't show every extreme that they name: `polymer_identifiers`: non-decreasing along the residues. `sequence_position_ids`: strictly increasing within a chain.
All inputs are finite; a program needn't handle non-finite values. No bound on the sum of `sequence_present_flags` on one device may be relied on, other than what follows from the above.
Results may differ from the reference program's by a relative error of at most 0.025.
Values may be sent and summed in bfloat16 or wider, within the bound.
No kernel may reach another device: no remote copies, remote signals or barrier semaphores. Data moves between devices by JAX's collectives and lax.ppermute only.
A program may use at most 192 MiB of HBM per device.

```python
import math
import jax
import jax.numpy as jnp
from jax import lax

SEQUENCE_DEPTH = 64
ATTENTION_HEADS = 8
HEAD_SIZE = 8
CZ = 128
HEAD_PRODUCT = 64
SEQUENCE_TOTAL = 256
CROP_LENGTH = 2048
CHAINS = 4
RMAX = 32
BINS = 66
N_ROW = 8


def chain_layout(key):
    quarter = CROP_LENGTH // (4 * CHAINS)
    shifts = jax.random.randint(jax.random.fold_in(key, 11), (CHAINS - 1,), -quarter, quarter + 1)
    bounds = jnp.arange(1, CHAINS, dtype=jnp.int32) * CROP_LENGTH // CHAINS + shifts
    position = jnp.arange(CROP_LENGTH, dtype=jnp.int32)
    chain = jnp.sum((position[:, None] >= bounds[None, :]).astype(jnp.int32), axis=1).astype(jnp.int32)
    begins = jnp.concatenate([jnp.zeros((1,), jnp.int32), bounds.astype(jnp.int32)])
    chain_start = begins[chain]
    first = jax.random.randint(jax.random.fold_in(key, 12), (CHAINS,), 1, 200)
    skipped = (jax.random.randint(jax.random.fold_in(key, 13), (CROP_LENGTH,), 0, 8) == 0).astype(jnp.int32)
    gaps = skipped * jax.random.randint(jax.random.fold_in(key, 14), (CROP_LENGTH,), 1, 20)
    climbed = jnp.cumsum(gaps).astype(jnp.int32)
    index = first[chain] + (position - chain_start) + climbed - climbed[chain_start]
    index = index + (20 * CROP_LENGTH + 199 - jnp.max(index))
    return (chain, index.astype(jnp.int32))


def draw_polymer_identifiers(key, part):
    layout = chain_layout(key)
    return layout[0]


def draw_sequence_position_ids(key, part):
    layout = chain_layout(key)
    return layout[1]


def draw_sequence_stack(key, part):
    key = jax.random.fold_in(key, 1)
    random_seeds = jax.random.split(key, 3)
    feature_axis = jnp.exp(jax.random.uniform(random_seeds[0], (SEQUENCE_DEPTH,), jnp.float32, 0.0, math.log(10.0)))
    sequence_factors = 0.1 * jnp.exp(jax.random.uniform(random_seeds[1], (SEQUENCE_TOTAL, 1, 1), jnp.float32, 0.0, math.log(10.0)))
    starting_vector = jnp.clip(jax.random.normal(random_seeds[2], (SEQUENCE_TOTAL, CROP_LENGTH, SEQUENCE_DEPTH), jnp.float32), -4.0, 4.0)
    return (starting_vector * feature_axis * sequence_factors).astype(jnp.bfloat16)


def draw_twofold_features(key, part):
    key = jax.random.fold_in(key, 2)
    random_seeds = jax.random.split(key, 3)
    feature_axis = jnp.exp(jax.random.uniform(random_seeds[0], (CZ,), jnp.float32, 0.0, math.log(10.0)))
    sequence_factors = 0.1 * jnp.exp(jax.random.uniform(random_seeds[1], (CROP_LENGTH, 1, 1), jnp.float32, 0.0, math.log(10.0)))
    starting_vector = jnp.clip(jax.random.normal(random_seeds[2], (CROP_LENGTH, CROP_LENGTH, CZ), jnp.float32), -4.0, 4.0)
    return (starting_vector * feature_axis * sequence_factors).astype(jnp.bfloat16)


def draw_separation_bucket_shift(key, part):
    key = jax.random.fold_in(key, 3)
    random_seeds = jax.random.split(key, 1)
    starting_vector = jnp.clip(jax.random.normal(random_seeds[0], (BINS, ATTENTION_HEADS), jnp.float32), -4.0, 4.0)
    return starting_vector


def touch_ends(drawn, stream_key, least, top_value):
    longest = drawn.shape.index(max(drawn.shape))
    spots = []
    for shift in (0, 1):
        where = [jax.random.randint(jax.random.fold_in(stream_key, axis), (), 0, length) for axis, length in enumerate(drawn.shape)]
        where[longest] = (where[longest] + shift) % drawn.shape[longest]
        spots.append(tuple(where))
    return drawn.at[spots[0]].set(least).at[spots[1]].set(top_value)


def block_levels(key, extent, cuts, least, largest):
    factor_of, own = 1.0, jax.random.fold_in(key, 6)
    for dim, shards_of in cuts:
        heights = jnp.exp(jax.random.uniform(jax.random.fold_in(own, dim), (shards_of,), jnp.float32, least / len(cuts), largest / len(cuts)))
        factor_of = factor_of * jnp.repeat(heights, extent[dim] // shards_of).reshape([-1 if axis == dim else 1 for axis in range(len(extent))])
    return factor_of


def gaussian(key, shape, deviation, limit, cuts=(), kind=jnp.bfloat16):
    level = block_levels(key, shape, cuts, -0.22, 0.18) if cuts else 1.0
    values = jax.random.normal(key, shape, jnp.float32) * deviation * level
    return jnp.minimum(jnp.maximum(values, -limit), limit).astype(kind)


def setup_inputs(seed: int = 0) -> dict:
    key_of = jax.random.split(jax.random.key(seed), 14)
    return {
        "sequence_stack": draw_sequence_stack(jax.random.fold_in(key_of[13], 71), 0),
        "twofold_features": draw_twofold_features(jax.random.fold_in(key_of[13], 71), 0),
        "incoming_adjoint": gaussian(key_of[2], (SEQUENCE_TOTAL, CROP_LENGTH, SEQUENCE_DEPTH), 1.0, 6.0, ((0, 8), (1, 32))),
        "sequence_present_flags": touch_ends((jax.random.randint(key_of[3], (SEQUENCE_TOTAL,), 0, 8) < 7).astype(jnp.int32), jax.random.fold_in(key_of[3], 1), 0, 1),
        "polymer_identifiers": draw_polymer_identifiers(jax.random.fold_in(key_of[13], 71), 0),
        "sequence_position_ids": draw_sequence_position_ids(jax.random.fold_in(key_of[13], 71), 0),
        "sequence_stack_multiplier": jnp.clip(1.0 + 0.15 * jax.random.normal(key_of[6], (SEQUENCE_DEPTH,), jnp.float32), 0.25, 1.75),
        "twofold_stack_multiplier": jnp.clip(1.0 + 0.15 * jax.random.normal(key_of[7], (CZ,), jnp.float32), 0.25, 1.75),
        "content_projection": gaussian(key_of[8], (SEQUENCE_DEPTH, HEAD_PRODUCT), SEQUENCE_DEPTH ** -0.5, 0.75),
        "sigmoid_projection": gaussian(key_of[9], (SEQUENCE_DEPTH, HEAD_PRODUCT), SEQUENCE_DEPTH ** -0.5, 0.75),
        "final_projection": gaussian(key_of[10], (HEAD_PRODUCT, SEQUENCE_DEPTH), HEAD_PRODUCT ** -0.5, 0.75),
        "twofold_head_projection": gaussian(key_of[11], (CZ, ATTENTION_HEADS), CZ ** -0.5, 0.5, (), jnp.float32),
        "separation_bucket_shift": draw_separation_bucket_shift(jax.random.fold_in(key_of[13], 71), 0),
    }


eps = 1e-05
exact = lax.Precision.HIGHEST

def standardize_features(field, gain):
    center = field - lax.optimization_barrier(jnp.mean(field, -1, keepdims=True))
    scale = lax.rsqrt(lax.optimization_barrier(jnp.mean(center * center, -1, keepdims=True)) + eps)
    normed = center * scale
    return (normed * gain, normed, scale)

def layer_norm_backward(grad, normed, scale, gain):
    scaled = grad * gain
    return scale * (scaled - lax.optimization_barrier(jnp.mean(scaled, -1, keepdims=True)) - normed * lax.optimization_barrier(jnp.mean(scaled * normed, -1, keepdims=True)))

def offset_bins(chain_rows, chain_cols, index_rows, index_cols):
    offset = jnp.clip(index_rows[:, None] - index_cols[None, :] + RMAX, 0, 2 * RMAX)
    return jnp.where(chain_rows[:, None] == chain_cols[None, :], offset, 2 * RMAX + 1).astype(jnp.int32)

def pair_logits(tile, twofold_stack_multiplier, twofold_head_projection, separation_bucket_shift, bins):
    shifted, normed, scale = standardize_features(tile.astype(jnp.float32), twofold_stack_multiplier)
    onehot = (bins[:, :, None] == jnp.arange(BINS, dtype=jnp.int32)[None, None, :]).astype(jnp.float32)
    logits = jnp.einsum('ijc,ch->hij', shifted, twofold_head_projection, precision=exact)
    return logits + jnp.einsum('ijk,kh->hij', onehot, separation_bucket_shift, precision=exact)

def reference(sequence_stack, twofold_features, incoming_adjoint, sequence_present_flags, polymer_identifiers, sequence_position_ids, sequence_stack_multiplier, twofold_stack_multiplier, content_projection, sigmoid_projection, final_projection, twofold_head_projection, separation_bucket_shift):
    thirtytwo_bit_type = jnp.float32
    sequence_minus_mean, standardized_sequences, sequence_stack_factor = standardize_features(sequence_stack.astype(thirtytwo_bit_type), sequence_stack_multiplier)
    alignment_normalized = sequence_minus_mean.astype(jnp.bfloat16)
    content_every_sequence = jnp.einsum('umv,vw->umw', alignment_normalized.astype(thirtytwo_bit_type), content_projection.astype(thirtytwo_bit_type)).astype(jnp.bfloat16)
    gate_activation = jax.nn.sigmoid(jnp.einsum('umv,vw->umw', alignment_normalized.astype(thirtytwo_bit_type), sigmoid_projection.astype(thirtytwo_bit_type)))
    masked_logits = incoming_adjoint.astype(thirtytwo_bit_type) * sequence_present_flags.astype(thirtytwo_bit_type)[:, None, None]
    upstream = jnp.einsum('snc,dc->snd', masked_logits, final_projection.astype(thirtytwo_bit_type))
    increment_tensor = (gate_activation * upstream).astype(jnp.bfloat16)
    block = CROP_LENGTH // N_ROW
    starts = jnp.arange(N_ROW, dtype=jnp.int32) * block
    pair_blocks = twofold_features.reshape(N_ROW, block, CROP_LENGTH, CZ)

    def forward_block(item):
        tile, start = item
        bins = offset_bins(lax.dynamic_slice_in_dim(polymer_identifiers, start, block), polymer_identifiers, lax.dynamic_slice_in_dim(sequence_position_ids, start, block), sequence_position_ids)
        logits = pair_logits(tile, twofold_stack_multiplier, twofold_head_projection, separation_bucket_shift, bins)
        peak = lax.optimization_barrier(jnp.max(logits, -1, keepdims=True))
        raised = jnp.exp(logits - peak)
        return (raised / lax.optimization_barrier(jnp.sum(raised, -1, keepdims=True))).astype(jnp.bfloat16)
    weight_blocks = lax.map(forward_block, (pair_blocks, starts))
    attention_probabilities = weight_blocks.transpose(1, 0, 2, 3).reshape(ATTENTION_HEADS, CROP_LENGTH, CROP_LENGTH).astype(thirtytwo_bit_type)
    content_per_head = content_every_sequence.astype(thirtytwo_bit_type).reshape(SEQUENCE_TOTAL, CROP_LENGTH, ATTENTION_HEADS, HEAD_SIZE)
    increment_per_head = increment_tensor.astype(thirtytwo_bit_type).reshape(SEQUENCE_TOTAL, CROP_LENGTH, ATTENTION_HEADS, HEAD_SIZE)
    attended_result = jnp.einsum('azg,lgak->lzak', attention_probabilities, content_per_head).reshape(SEQUENCE_TOTAL, CROP_LENGTH, HEAD_PRODUCT)
    gate_grad = (upstream * attended_result * gate_activation * (1.0 - gate_activation)).astype(jnp.bfloat16)
    content_adjoint = jnp.einsum('ozk,azof->akof', attention_probabilities, increment_per_head).reshape(SEQUENCE_TOTAL, CROP_LENGTH, HEAD_PRODUCT).astype(jnp.bfloat16)
    normalized_gradient = jnp.einsum('snd,cd->snc', content_adjoint.astype(thirtytwo_bit_type), content_projection.astype(thirtytwo_bit_type))
    normalized_gradient = normalized_gradient + jnp.einsum('snd,cd->snc', gate_grad.astype(thirtytwo_bit_type), sigmoid_projection.astype(thirtytwo_bit_type))
    alignment_gradient = layer_norm_backward(normalized_gradient, standardized_sequences, sequence_stack_factor, sequence_stack_multiplier).astype(jnp.bfloat16)
    scores = jnp.einsum('sihc,sjhc->hij', increment_per_head, content_per_head)
    score_blocks = scores.reshape(ATTENTION_HEADS, N_ROW, block, CROP_LENGTH).transpose(1, 0, 2, 3)

    def backward_block(item):
        tile, score_tile, weight_tile = item
        shifted, normed, scale = standardize_features(tile.astype(thirtytwo_bit_type), twofold_stack_multiplier)
        chosen = weight_tile.astype(thirtytwo_bit_type)
        row_total = lax.optimization_barrier(jnp.sum(chosen * score_tile, -1, keepdims=True))
        logit_grad = chosen * (score_tile - row_total)
        shifted_grad = jnp.einsum('hij,ch->ijc', logit_grad, twofold_head_projection, precision=exact)
        return layer_norm_backward(shifted_grad, normed, scale, twofold_stack_multiplier).astype(jnp.bfloat16)
    pair_gradient = lax.map(backward_block, (pair_blocks, score_blocks, weight_blocks)).reshape(CROP_LENGTH, CROP_LENGTH, CZ)
    return (alignment_gradient, pair_gradient)
```

```python
import functools

import jax
import jax.numpy as jnp
from jax import lax
from jax.experimental import pallas as pl
from jax.experimental.pallas import tpu as pltpu
from jax.sharding import Mesh
from jax.sharding import PartitionSpec as P

RMAX = 32
EPS = 1e-05
BF = jnp.bfloat16
F32 = jnp.float32
VMEM = pltpu.CompilerParams(vmem_limit_bytes=48 * 1024 * 1024)
HALF = 64


def mm(a, b):
    return lax.dot_general(a, b, (((1,), (0,)), ((), ())), preferred_element_type=F32)


def mm_nt(a, b):
    return lax.dot_general(a, b, (((1,), (1,)), ((), ())), preferred_element_type=F32)


def mm_tn(a, b):
    return lax.dot_general(a, b, (((0,), (0,)), ((), ())), preferred_element_type=F32)


def iota(shape, dim):
    return lax.broadcasted_iota(jnp.int32, shape, dim)


def split3(x):
    hi = x.astype(BF).astype(F32)
    mid = (x - hi).astype(BF).astype(F32)
    return hi, mid, x - hi - mid


def spread(weight, transposed, out_ref):
    k, l = iota((64, 1024), 0), iota((64, 1024), 1)
    pick = jnp.where((k // 8 == l // 128) & (k % 8 == l % 8), 1.0, 0.0).astype(BF)
    wide = mm_tn(weight, pick) if transposed else mm(weight, pick)
    owner = (l % 128) // 8
    for s in range(16):
        out_ref[s * 64 : (s + 1) * 64, :] = jnp.where(owner == s, wide, 0.0).astype(BF)


def standardize(x):
    center = x - jnp.mean(x, -1, keepdims=True)
    scale = lax.rsqrt(jnp.mean(center * center, -1, keepdims=True) + EPS)
    return center * scale, scale


def msa_forward(flags, msa, adj, gain, wc, ws, wf, u_out, v_out, t_out, bdc, bds, bdf):
    spread(wc[...], False, bdc)
    spread(ws[...], False, bds)
    spread(wf[...], True, bdf)
    g = gain[...]
    for d in range(2):
        normed, masked = [], []
        for s in range(16):
            row = d * 16 + s
            normed.append((standardize(msa[row].astype(F32))[0] * g).astype(BF))
            masked.append((adj[row].astype(F32) * flags[row].astype(F32)).astype(BF))
        x = jnp.concatenate(normed, axis=1)
        y = jnp.concatenate(masked, axis=1)
        values = mm(x, bdc[...]).astype(BF)
        gate = jax.nn.sigmoid(mm(x, bds[...]))
        upstream = mm(y, bdf[...])
        moved = gate * upstream
        update = moved.astype(BF)
        tail = moved * (1.0 - gate)
        for h in range(8):
            cols = slice(h * 128, (h + 1) * 128)
            v_out[h, d] = values[:, cols]
            t_out[h, d] = tail[:, cols]
            for b in range(4):
                u_out[h, d, b] = update[:, cols]


def partner(x, k, lane):
    return jnp.where(lane & k == 0, pltpu.roll(x, 128 - k, 1), pltpu.roll(x, k, 1))


def pair_forward(pair, bins, proj, table, v_in, out, saved, p_s, m_s):
    w_hi, w_mid, w_lo = split3(proj[...])
    ones8 = jnp.full((8, 128), 1.0 / 128, F32)
    lhs = jnp.concatenate([w_hi, w_mid, w_lo, ones8], axis=0).astype(BF)
    ones8 = ones8.astype(BF)
    averager = jnp.full((128, 128), 1.0 / 128, F32).astype(BF)
    b_lhs = jnp.concatenate(list(split3(table[...])) + [jnp.zeros((8, 128), F32)], axis=0).astype(BF)
    lane = iota((8, 128), 1)
    klass = iota((128, 1024), 0)
    for g in range(4):
        x = jnp.concatenate(
            [pair[e * 32 + g * 8 + rho] for rho in range(8) for e in range(2)], axis=0
        )
        center = x.astype(F32) - mm(x, averager)
        square = center * center
        s_hi = square.astype(BF)
        s_lo = (square - s_hi.astype(F32)).astype(BF)
        var = mm_nt(ones8, s_hi) + mm_nt(ones8, s_lo)
        z = mm_nt(lhs, x)
        scale = lax.rsqrt(var + EPS)
        t = (z[0:8] + z[8:16] + z[16:24]) * scale
        saved[g, 0:8, :] = t
        saved[g, 8:16, :] = scale
        saved[g, 16:24, :] = z[24:32]
        onehot = jnp.where(klass == bins[g], 1.0, 0.0).astype(BF)
        zb = mm(b_lhs, onehot)
        logits = t + (zb[0:8] + zb[8:16] + zb[16:24])
        for rho in range(8):
            part = logits[:, rho * 128 : (rho + 1) * 128]
            top = part
            for k in (1, 2, 4, 8, 16, 32):
                top = jnp.maximum(top, partner(top, k, lane))
            top = top.astype(BF).astype(F32)
            p_s[:, g * 8 + rho, :] = jnp.exp(part - top)
            m_s[:, g * 8 + rho, :] = top
    quarter = iota((16, 128), 1) // 32
    for h in range(8):
        weights = p_s[h].astype(BF)
        low, high = m_s[h, 0:16, :], m_s[h, 16:32, :]
        packed = jnp.where(
            quarter == 0,
            low,
            jnp.where(
                quarter == 1, pltpu.roll(low, 64, 1), jnp.where(quarter == 2, pltpu.roll(high, 64, 1), high)
            ),
        ).astype(BF)
        for d in range(2):
            out[h, d, 0, 0:64, :] = v_in[h, d]
            out[h, d, 0, 64:96, :] = weights
            out[h, d, 0, 96:112, :] = packed


def merge_products(ub, vw, p_out, stats, m_s):
    lane = iota((128, 128), 1)
    quarter = lane // 32
    left = lane < HALF
    for half in range(2):
        tops = []
        for c in range(8):
            q = vw[:, c, 96:112, :].astype(F32).reshape(128, 128)
            q64 = pltpu.roll(q, 64, 1)
            if half == 0:
                tops.append(jnp.where(quarter == 0, q, jnp.where(quarter == 3, q64, pltpu.roll(q, 32, 1))))
            else:
                tops.append(jnp.where(quarter == 0, q64, jnp.where(quarter == 3, q, pltpu.roll(q, 96, 1))))
        peak = functools.reduce(jnp.maximum, tops)
        crossed = pltpu.roll(peak, 64, 1)
        m_s[:, 0, half] = jnp.where(left, peak, crossed).reshape(8, 16, 128)
        m_s[:, 1, half] = jnp.where(left, crossed, peak).reshape(8, 16, 128)
        rows = slice(64 + half * 16, 80 + half * 16)
        for cp in range(4):
            one, two = [
                vw[:, c, rows, :].astype(F32).reshape(128, 128) * jnp.exp(tops[c] - peak)
                for c in (2 * cp, 2 * cp + 1)
            ]
            cols = slice(cp * 128, (cp + 1) * 128)
            even = jnp.where(left, one, pltpu.roll(two, 64, 1)).astype(BF)
            odd = jnp.where(left, pltpu.roll(one, 64, 1), two).astype(BF)
            p_out[:, 0, half, :, cols] = even.reshape(8, 16, 128)
            p_out[:, 1, half, :, cols] = odd.reshape(8, 16, 128)
    p = p_out[...].reshape(512, 512)
    total = mm(p, jnp.full((512, 128), 1.0, F32).astype(BF))
    acc = jnp.zeros((512, 128), F32)
    for r in range(0, 8, 2):
        v = jnp.concatenate([vw[r + k, :, 0:64, :].reshape(512, 128) for k in range(2)], axis=1)
        c = mm(p, v)
        for k in range(2):
            acc += ub[r + k].reshape(512, 128).astype(F32) * c[:, k * 128 : (k + 1) * 128]
    score = jnp.sum(acc, axis=1, keepdims=True)
    column = iota((512, 128), 1)
    mixed = jnp.where(
        column == 0,
        m_s[...].reshape(512, 128),
        jnp.where(column == 1, total, jnp.where(column == 2, score, 0.0)),
    )
    rows = jnp.transpose(mixed)[0:8]
    for k in range(8):
        stats[k] = rows


def score_products(ub, vw, out):
    acc = jnp.zeros((512, 512), F32)
    for r in range(0, 8, 2):
        u = jnp.concatenate([ub[r + k].reshape(512, 128) for k in range(2)], axis=1)
        v = jnp.concatenate([vw[r + k, :, 0:64, :].reshape(512, 128) for k in range(2)], axis=1)
        acc += mm_nt(u, v)
    out[...] = acc


def gradients(stats, own, p_in, ub, scores, p_out, out):
    tops, totals, sums = stats[:, 0, :], stats[:, 1, :], stats[:, 2, :]
    peak = jnp.max(tops, axis=0, keepdims=True)
    factor = jnp.exp(tops - peak)
    total = 0.5 * jnp.sum(factor * totals, axis=0, keepdims=True)
    row_total = jnp.sum(factor * sums, axis=0, keepdims=True) / total
    mine = jnp.exp(own[0:1, :] - peak) / total
    which = iota((8, 512), 0)
    columns = jnp.transpose(jnp.where(which == 0, mine, jnp.where(which == 1, 0.5 * row_total, 0.0)))
    p = (p_in[...].reshape(512, 512).astype(F32) * columns[:, 0:1]).astype(BF)
    p_out[...] = p
    grad = (p.astype(F32) * (scores[...] - columns[:, 1:2])).reshape(8, 2, 32, 512)
    left = iota((256, 128), 1) < HALF
    for cp in range(4):
        cols = slice(cp * 128, (cp + 1) * 128)
        even, odd = [grad[:, e, :, cols].reshape(256, 128) for e in range(2)]
        one = jnp.where(left, even, pltpu.roll(odd, 64, 1)).astype(BF)
        two = jnp.where(left, pltpu.roll(even, 64, 1), odd).astype(BF)
        out[:, 2 * cp, 64:96, :] = one.reshape(8, 32, 128)
        out[:, 2 * cp + 1, 64:96, :] = two.reshape(8, 32, 128)
    pt = jnp.transpose(p)
    for r in range(0, 8, 2):
        u = jnp.concatenate([ub[r + k].reshape(512, 128) for k in range(2)], axis=1)
        grad_v = mm(pt, u).astype(BF)
        for k in range(2):
            out[r + k, :, 0:64, :] = grad_v[:, k * 128 : (k + 1) * 128].reshape(8, 64, 128)


def context_products(p, vw, out):
    for r in range(0, 8, 2):
        v = jnp.concatenate([vw[r + k, :, 0:64, :].reshape(512, 128) for k in range(2)], axis=1)
        c = mm(p[...], v).astype(BF)
        for k in range(2):
            out[r + k] = c[:, k * 128 : (k + 1) * 128].reshape(8, 64, 128)


def pair_backward(pair, grads, saved, proj, out, g_s):
    w_hi, w_mid, _ = split3(proj[...])
    row = iota((8, 128), 0)
    flag = jnp.where(row < 3, 1.0, 0.0)
    rhs = jnp.concatenate([w_hi, w_hi, w_mid, flag], axis=0).astype(BF)
    rhs_a = jnp.concatenate([flag, jnp.zeros((8, 128), F32)], axis=0).astype(BF)
    g_s[...] = grads[:, 0, 0].astype(F32) + grads[:, 1, 0].astype(F32)
    which = iota((8, 1024), 0)

    def stacked(x):
        hi, mid, low = split3(x)
        return jnp.where(which == 0, hi, jnp.where(which == 1, mid, jnp.where(which == 2, low, 0.0)))

    for g in range(4):
        grad = jnp.concatenate([g_s[:, g * 8 + rho, :] for rho in range(8)], axis=1)
        t, scale, mean = saved[g, 0:8, :], saved[g, 8:16, :], saved[g, 16:24, :]
        slope = jnp.sum(grad * t, axis=0, keepdims=True) * (1.0 / 128)
        alpha = scale * scale * slope
        scaled = grad * scale
        hi = scaled.astype(BF).astype(F32)
        lhs = jnp.concatenate([hi, scaled - hi, hi, stacked(alpha * mean)], axis=0).astype(BF)
        lhs_a = jnp.concatenate([stacked(alpha), jnp.zeros((8, 1024), F32)], axis=0).astype(BF)
        base = mm_tn(lhs, rhs)
        steep = mm_tn(lhs_a, rhs_a)
        for rho in range(8):
            for e in range(2):
                i = e * 32 + g * 8 + rho
                rows = slice((rho * 2 + e) * 64, (rho * 2 + e + 1) * 64)
                out[i] = (base[rows] - steep[rows] * pair[i].astype(F32)).astype(BF)


def msa_backward(msa, gain, wc, ws, gb, cb, tail, out, bdc, bds):
    spread(wc[...], False, bdc)
    spread(ws[...], False, bds)
    g = gain[...]
    for d in range(2):
        value_grad, gate_grad = [], []
        for h in range(8):
            total = gb[h, d, 0, 0:64, :].astype(F32)
            context = cb[h, d, 0].astype(F32)
            for k in range(1, 4):
                total += gb[h, d, k, 0:64, :].astype(F32)
                context += cb[h, d, k].astype(F32)
            value_grad.append(total.astype(BF))
            gate_grad.append((tail[h, d] * context).astype(BF))
        grad = mm_nt(jnp.concatenate(value_grad, axis=1), bdc[...])
        grad += mm_nt(jnp.concatenate(gate_grad, axis=1), bds[...])
        for s in range(16):
            row = d * 16 + s
            normed, scale = standardize(msa[row].astype(F32))
            scaled = grad[:, s * 64 : (s + 1) * 64] * g
            out[row] = (
                scale
                * (
                    scaled
                    - jnp.mean(scaled, -1, keepdims=True)
                    - normed * jnp.mean(scaled * normed, -1, keepdims=True)
                )
            ).astype(BF)


def exchange(x, axes):
    return lax.all_to_all(x, axes, 0, 0, tiled=True)


def shape(dims, dtype):
    return jax.ShapeDtypeStruct(dims, dtype)


def shards(msa, pair, adj, flags, chains, positions, msa_gain, pair_gain, wc, ws, wf, wp, table):
    vm = pl.BlockSpec(memory_space=pltpu.VMEM)
    sm = pl.BlockSpec(memory_space=pltpu.SMEM)
    gp, gq = ("row", "d", "a"), ("row", "d", "b")
    gain = msa_gain.reshape(1, 64)

    u_send, values, tail = pl.pallas_call(
        msa_forward,
        out_shape=(shape((8, 2, 4, 64, 128), BF), shape((8, 2, 64, 128), BF), shape((8, 2, 64, 128), F32)),
        in_specs=[sm] + [vm] * 6,
        out_specs=(vm, vm, vm),
        scratch_shapes=[pltpu.VMEM((1024, 1024), BF)] * 3,
        compiler_params=VMEM,
        name="msa_forward",
    )(flags, msa, adj, gain, wc, ws, wf)
    ub = exchange(u_send.reshape(64, 64, 128), gq).reshape(8, 8, 64, 128)

    row = lax.axis_index("row")
    col = lax.axis_index("d") * 16 + lax.axis_index("b") * 4 + lax.axis_index("a")

    def rows_of(x):
        return lax.dynamic_slice_in_dim(x, row * 256, 256).reshape(4, 2, 4, 8).transpose(0, 2, 3, 1)

    def cols_of(x):
        return lax.dynamic_slice_in_dim(x, col * 64, 64)

    offset = jnp.clip(rows_of(positions)[..., None] - cols_of(positions) + RMAX, 0, 2 * RMAX)
    bins = jnp.where(rows_of(chains)[..., None] == cols_of(chains), offset, 2 * RMAX + 1)
    bins = bins.reshape(16, 1, 1024)
    scaled = (wp * pair_gain[:, None]).T
    proj = scaled - jnp.mean(scaled, -1, keepdims=True)
    table_t = jnp.pad(table.T, ((0, 0), (0, 128 - table.shape[0])))

    def const(*dims):
        return pl.BlockSpec(dims, lambda k: (0,) * len(dims))

    vw_send, saved = pl.pallas_call(
        pair_forward,
        grid=(4,),
        out_shape=(shape((8, 2, 4, 112, 128), BF), shape((16, 24, 1024), F32)),
        in_specs=[
            pl.BlockSpec((64, 64, 128), lambda k: (k, 0, 0)),
            pl.BlockSpec((4, 1, 1024), lambda k: (k, 0, 0)),
            const(8, 128),
            const(8, 128),
            const(8, 2, 64, 128),
        ],
        out_specs=(
            pl.BlockSpec((8, 2, 1, 112, 128), lambda k: (0, 0, k, 0, 0)),
            pl.BlockSpec((4, 24, 1024), lambda k: (k, 0, 0)),
        ),
        scratch_shapes=[pltpu.VMEM((8, 32, 128), F32)] * 2,
        compiler_params=VMEM,
        name="pair_forward",
    )(pair, bins, proj, table_t, values)
    vw = exchange(vw_send.reshape(64, 112, 128), gp).reshape(8, 8, 112, 128)

    p_raw, stats = pl.pallas_call(
        merge_products,
        out_shape=(shape((8, 2, 2, 16, 512), BF), shape((8, 8, 512), F32)),
        in_specs=[vm, vm],
        out_specs=(vm, vm),
        scratch_shapes=[pltpu.VMEM((8, 2, 2, 16, 128), F32)],
        compiler_params=VMEM,
        name="merge_products",
    )(ub, vw)
    all_stats = exchange(stats, ("d", "b"))
    scores = pl.pallas_call(
        score_products,
        out_shape=shape((512, 512), F32),
        in_specs=[vm, vm],
        out_specs=vm,
        compiler_params=VMEM,
        name="score_products",
    )(ub, vw)
    p, gd_send = pl.pallas_call(
        gradients,
        out_shape=(shape((512, 512), BF), shape((8, 8, 96, 128), BF)),
        in_specs=[vm] * 5,
        out_specs=(vm, vm),
        compiler_params=VMEM,
        name="gradients",
    )(all_stats, stats[0], p_raw, ub, scores)
    gd = exchange(gd_send.reshape(64, 96, 128), gp).reshape(8, 2, 4, 96, 128)
    c_send = pl.pallas_call(
        context_products,
        out_shape=shape((8, 8, 64, 128), BF),
        in_specs=[vm, vm],
        out_specs=vm,
        compiler_params=VMEM,
        name="context_products",
    )(p, vw)
    cb = exchange(c_send.reshape(64, 64, 128), gq).reshape(8, 2, 4, 64, 128)
    pair_gradient = pl.pallas_call(
        pair_backward,
        grid=(4,),
        out_shape=shape((256, 64, 128), BF),
        in_specs=[
            pl.BlockSpec((64, 64, 128), lambda k: (k, 0, 0)),
            pl.BlockSpec((8, 2, 1, 32, 128), lambda k: (0, 0, k, 2, 0)),
            pl.BlockSpec((4, 24, 1024), lambda k: (k, 0, 0)),
            const(8, 128),
        ],
        out_specs=pl.BlockSpec((64, 64, 128), lambda k: (k, 0, 0)),
        scratch_shapes=[pltpu.VMEM((8, 32, 128), F32)],
        compiler_params=VMEM,
        name="pair_backward",
    )(pair, gd, saved, proj)
    alignment_gradient = pl.pallas_call(
        msa_backward,
        out_shape=shape((32, 64, 64), BF),
        in_specs=[vm] * 7,
        out_specs=vm,
        scratch_shapes=[pltpu.VMEM((1024, 1024), BF)] * 2,
        compiler_params=VMEM,
        name="msa_backward",
    )(msa, gain, wc, ws, gd, cb, tail)
    return (alignment_gradient, pair_gradient)


def solution(mesh):
    inner = Mesh(mesh.devices.reshape(8, 2, 4, 4), ("row", "d", "b", "a"))
    res = ("d", "b", "a")
    split = P("row", res, None)
    return jax.shard_map(
        shards,
        mesh=inner,
        in_specs=(split, split, split, P("row")) + (P(),) * 9,
        out_specs=(split, split),
        check_vma=False,
    )
```

```python
import functools

import jax
import jax.numpy as jnp
from jax import lax
from jax.experimental import pallas as pl
from jax.experimental.pallas import tpu as pltpu
from jax.sharding import Mesh
from jax.sharding import PartitionSpec as P

RMAX = 32
EPS = 1e-05
BF = jnp.bfloat16
F32 = jnp.float32
VMEM = pltpu.CompilerParams(vmem_limit_bytes=48 * 1024 * 1024)
WHOLE = pltpu.CompilerParams(vmem_limit_bytes=60 * 1024 * 1024)
HALF = 64


def mm(a, b):
    return lax.dot_general(a, b, (((1,), (0,)), ((), ())), preferred_element_type=F32)


def mm_nt(a, b):
    return lax.dot_general(a, b, (((1,), (1,)), ((), ())), preferred_element_type=F32)


def mm_tn(a, b):
    return lax.dot_general(a, b, (((0,), (0,)), ((), ())), preferred_element_type=F32)


def iota(shape, dim):
    return lax.broadcasted_iota(jnp.int32, shape, dim)


def split3(x):
    hi = x.astype(BF).astype(F32)
    mid = (x - hi).astype(BF).astype(F32)
    return hi, mid, x - hi - mid


def spread(weight, transposed, out_ref):
    k, l = iota((64, 1024), 0), iota((64, 1024), 1)
    pick = jnp.where((k // 8 == l // 128) & (k % 8 == l % 8), 1.0, 0.0).astype(BF)
    wide = mm_tn(weight, pick) if transposed else mm(weight, pick)
    owner = (l % 128) // 8
    for s in range(16):
        out_ref[s * 64 : (s + 1) * 64, :] = jnp.where(owner == s, wide, 0.0).astype(BF)


def averager():
    half = (iota((128, 128), 0) < 64) == (iota((128, 128), 1) < 64)
    return jnp.where(half, 1.0 / 64, 0.0).astype(BF)


def half_means(x, ones):
    hi = x.astype(BF)
    return mm(hi, ones) + mm((x - hi.astype(F32)).astype(BF), ones)


def paired(x):
    return jnp.concatenate([jnp.concatenate([x(2 * k), x(2 * k + 1)], axis=1) for k in range(16)], axis=0)


def beside(x, d):
    return jnp.concatenate([x[(d * 8 + k) * 64 : (d * 8 + k + 1) * 64] for k in range(8)], axis=1)


def standardize(x, ones):
    center = x.astype(F32) - mm(x, ones)
    scale = lax.rsqrt(half_means(center * center, ones) + EPS)
    return center * scale, scale


def twice(gain):
    return jnp.concatenate([gain[...], gain[...]], axis=1)


def msa_updates(flags, msa, adj, gain, ws, wf, u_out, t_out, bds, bdf):
    spread(ws[...], False, bds)
    spread(wf[...], True, bdf)
    normed, _ = standardize(paired(lambda s: msa[s]), averager())
    normed = (normed * twice(gain)).astype(BF)
    masked = paired(lambda s: (adj[s].astype(F32) * flags[s].astype(F32)).astype(BF))
    for d in range(2):
        gate = jax.nn.sigmoid(mm(beside(normed, d), bds[...]))
        moved = gate * mm(beside(masked, d), bdf[...])
        update = moved.astype(BF)
        tail = moved * (1.0 - gate)
        for h in range(8):
            cols = slice(h * 128, (h + 1) * 128)
            t_out[h, d] = tail[:, cols]
            for b in range(4):
                u_out[h, d, b] = update[:, cols]


def msa_values(msa, gain, wc, v_out, bdc):
    spread(wc[...], False, bdc)
    normed, _ = standardize(paired(lambda s: msa[s]), averager())
    normed = (normed * twice(gain)).astype(BF)
    for d in range(2):
        values = mm(beside(normed, d), bdc[...]).astype(BF)
        for h in range(8):
            v_out[h, d] = values[:, h * 128 : (h + 1) * 128]


def partner(x, k, lane):
    return jnp.where(lane & k == 0, pltpu.roll(x, 128 - k, 1), pltpu.roll(x, k, 1))


def pair_forward(pair, bins, proj, table, v_in, out, saved, p_s, m_s):
    w_hi, w_mid, w_lo = split3(proj[...])
    ones8 = jnp.full((8, 128), 1.0 / 128, F32)
    lhs = jnp.concatenate([w_hi, w_mid, w_lo, ones8], axis=0).astype(BF)
    ones8 = ones8.astype(BF)
    mean = jnp.full((128, 128), 1.0 / 128, F32).astype(BF)
    b_lhs = jnp.concatenate(list(split3(table[...])) + [jnp.zeros((8, 128), F32)], axis=0).astype(BF)
    lane = iota((8, 128), 1)
    klass = iota((128, 1024), 0)
    for g in range(4):
        x = jnp.concatenate(
            [pair[e * 32 + g * 8 + rho] for rho in range(8) for e in range(2)], axis=0
        )
        center = x.astype(F32) - mm(x, mean)
        square = center * center
        s_hi = square.astype(BF)
        s_lo = (square - s_hi.astype(F32)).astype(BF)
        var = mm_nt(ones8, s_hi) + mm_nt(ones8, s_lo)
        z = mm_nt(lhs, x)
        scale = lax.rsqrt(var + EPS)
        t = (z[0:8] + z[8:16] + z[16:24]) * scale
        saved[g, 0:8, :] = t
        saved[g, 8:16, :] = scale
        saved[g, 16:24, :] = z[24:32]
        onehot = jnp.where(klass == bins[g], 1.0, 0.0).astype(BF)
        zb = mm(b_lhs, onehot)
        logits = t + (zb[0:8] + zb[8:16] + zb[16:24])
        for rho in range(8):
            part = logits[:, rho * 128 : (rho + 1) * 128]
            top = part
            for k in (1, 2, 4, 8, 16, 32):
                top = jnp.maximum(top, partner(top, k, lane))
            top = top.astype(BF).astype(F32)
            p_s[:, g * 8 + rho, :] = jnp.exp(part - top)
            m_s[:, g * 8 + rho, :] = top
    quarter = iota((16, 128), 1) // 32
    for h in range(8):
        weights = p_s[h].astype(BF)
        low, high = m_s[h, 0:16, :], m_s[h, 16:32, :]
        packed = jnp.where(
            quarter == 0,
            low,
            jnp.where(
                quarter == 1, pltpu.roll(low, 64, 1), jnp.where(quarter == 2, pltpu.roll(high, 64, 1), high)
            ),
        ).astype(BF)
        for d in range(2):
            out[h, d, 0, 0:64, :] = v_in[h, d]
            out[h, d, 0, 64:96, :] = weights
            out[h, d, 0, 96:112, :] = packed


def merge_products(block, ub, vw, p_out, stats, c0, c1, c2, c3, m_s, c_s):
    lane = iota((128, 128), 1)
    quarter = lane // 32
    left = lane < HALF
    for half in range(2):
        tops = []
        for c in range(8):
            q = vw[:, c, 96:112, :].astype(F32).reshape(128, 128)
            q64 = pltpu.roll(q, 64, 1)
            if half == 0:
                tops.append(jnp.where(quarter == 0, q, jnp.where(quarter == 3, q64, pltpu.roll(q, 32, 1))))
            else:
                tops.append(jnp.where(quarter == 0, q64, jnp.where(quarter == 3, q, pltpu.roll(q, 96, 1))))
        peak = functools.reduce(jnp.maximum, tops)
        crossed = pltpu.roll(peak, 64, 1)
        m_s[:, 0, half] = jnp.where(left, peak, crossed).reshape(8, 16, 128)
        m_s[:, 1, half] = jnp.where(left, crossed, peak).reshape(8, 16, 128)
        rows = slice(64 + half * 16, 80 + half * 16)
        for cp in range(4):
            one, two = [
                vw[:, c, rows, :].astype(F32).reshape(128, 128) * jnp.exp(tops[c] - peak)
                for c in (2 * cp, 2 * cp + 1)
            ]
            cols = slice(cp * 128, (cp + 1) * 128)
            even = jnp.where(left, one, pltpu.roll(two, 64, 1)).astype(BF)
            odd = jnp.where(left, pltpu.roll(one, 64, 1), two).astype(BF)
            p_out[:, 0, half, :, cols] = even.reshape(8, 16, 128)
            p_out[:, 1, half, :, cols] = odd.reshape(8, 16, 128)
    p = p_out[...].reshape(512, 512)
    total = mm(p, jnp.full((512, 128), 1.0, F32).astype(BF))
    acc = jnp.zeros((512, 128), F32)
    for r in range(0, 8, 2):
        v = jnp.concatenate([vw[r + k, :, 0:64, :].reshape(512, 128) for k in range(2)], axis=1)
        c = mm(p, v)
        for k in range(2):
            part = c[:, k * 128 : (k + 1) * 128]
            acc += ub[r + k].reshape(512, 128).astype(F32) * part
            c_s[r + k] = part.astype(BF)
    score = jnp.sum(acc, axis=1, keepdims=True)
    column = iota((512, 128), 1)
    mixed = jnp.where(
        column == 0,
        m_s[...].reshape(512, 128),
        jnp.where(column == 1, total, jnp.where(column == 2, score, 0.0)),
    )
    stats[...] = jnp.transpose(mixed)[0:8]
    for k, out in enumerate((c0, c1, c2, c3)):
        for d in range(2):
            start = pl.multiple_of(d * 256 + (block[0] ^ k) * 64, 64)
            for r in range(8):
                out[r, d] = c_s[r, pl.ds(start, 64), :]


def score_products(ub, vw, out):
    acc = jnp.zeros((512, 512), F32)
    for r in range(0, 8, 2):
        u = jnp.concatenate([ub[r + k].reshape(512, 128) for k in range(2)], axis=1)
        v = jnp.concatenate([vw[r + k, :, 0:64, :].reshape(512, 128) for k in range(2)], axis=1)
        acc += mm_nt(u, v)
    out[...] = acc


def streamed(stats):
    rows = [x[...] for x in stats]
    peak = functools.reduce(jnp.maximum, [x[0:1] for x in rows])
    factor = [jnp.exp(x[0:1] - peak) for x in rows]
    total = sum(f * x[1:2] for f, x in zip(factor, rows))
    return [f / total for f in factor], rows


def gradients(own, first, second, third, p_in, ub, scores, *rest):
    out = rest[-1]
    share, rows = streamed((own, first, second, third))
    row_total = sum(f * x[2:3] for f, x in zip(share, rows))
    which = iota((8, 512), 0)
    columns = jnp.transpose(jnp.where(which == 0, share[0], jnp.where(which == 1, row_total, 0.0)))
    p = (p_in[...].reshape(512, 512).astype(F32) * columns[:, 0:1]).astype(BF)
    grad = (p.astype(F32) * (scores[...] - columns[:, 1:2])).reshape(8, 2, 32, 512)
    left = iota((256, 128), 1) < HALF
    for cp in range(4):
        cols = slice(cp * 128, (cp + 1) * 128)
        even, odd = [grad[:, e, :, cols].reshape(256, 128) for e in range(2)]
        one = jnp.where(left, even, pltpu.roll(odd, 64, 1)).astype(BF)
        two = jnp.where(left, pltpu.roll(even, 64, 1), odd).astype(BF)
        out[:, 2 * cp, 64:96, :] = one.reshape(8, 32, 128)
        out[:, 2 * cp + 1, 64:96, :] = two.reshape(8, 32, 128)
    pt = jnp.transpose(p)
    for r in range(0, 8, 2):
        u = jnp.concatenate([ub[r + k].reshape(512, 128) for k in range(2)], axis=1)
        grad_v = mm(pt, u).astype(BF)
        for k in range(2):
            out[r + k, :, 0:64, :] = grad_v[:, k * 128 : (k + 1) * 128].reshape(8, 64, 128)


def context_sum(block, own, first, second, third, c0, c1, c2, c3, out, f_s):
    share, _ = streamed((own, first, second, third))
    which = iota((8, 512), 0)
    mixed = jnp.zeros((8, 512), F32)
    for k in range(4):
        mixed = jnp.where(which == k, share[k], mixed)
    f_s[...] = jnp.transpose(mixed)
    for d in range(2):
        f = f_s[pl.ds(pl.multiple_of(d * 256 + block[0] * 64, 64), 64), :]
        for r in range(8):
            parts = [c[r, d].astype(F32) * f[:, k : k + 1] for k, c in enumerate((c0, c1, c2, c3))]
            out[r, d] = ((parts[0] + parts[1]) + (parts[2] + parts[3])).astype(BF)


def pair_backward(pair, grads, saved, proj, out, g_s):
    w_hi, w_mid, _ = split3(proj[...])
    row = iota((8, 128), 0)
    flag = jnp.where(row < 3, 1.0, 0.0)
    rhs = jnp.concatenate([w_hi, w_hi, w_mid, flag], axis=0).astype(BF)
    rhs_a = jnp.concatenate([flag, jnp.zeros((8, 128), F32)], axis=0).astype(BF)
    g_s[...] = grads[:, 0, 0].astype(F32) + grads[:, 1, 0].astype(F32)
    which = iota((8, 1024), 0)

    def stacked(x):
        hi, mid, low = split3(x)
        return jnp.where(which == 0, hi, jnp.where(which == 1, mid, jnp.where(which == 2, low, 0.0)))

    for g in range(4):
        grad = jnp.concatenate([g_s[:, g * 8 + rho, :] for rho in range(8)], axis=1)
        t, scale, mean = saved[g, 0:8, :], saved[g, 8:16, :], saved[g, 16:24, :]
        slope = jnp.sum(grad * t, axis=0, keepdims=True) * (1.0 / 128)
        alpha = scale * scale * slope
        scaled = grad * scale
        hi = scaled.astype(BF).astype(F32)
        lhs = jnp.concatenate([hi, scaled - hi, hi, stacked(alpha * mean)], axis=0).astype(BF)
        lhs_a = jnp.concatenate([stacked(alpha), jnp.zeros((8, 1024), F32)], axis=0).astype(BF)
        base = mm_tn(lhs, rhs)
        steep = mm_tn(lhs_a, rhs_a)
        for rho in range(8):
            for e in range(2):
                i = e * 32 + g * 8 + rho
                rows = slice((rho * 2 + e) * 64, (rho * 2 + e + 1) * 64)
                out[i] = (base[rows] - steep[rows] * pair[i].astype(F32)).astype(BF)


def msa_partial(msa, wc, gb, normed_out, scale_out, grad_out, bdc):
    spread(wc[...], False, bdc)
    normed, scale = standardize(paired(lambda s: msa[s]), averager())
    normed_out[...] = normed
    scale_out[...] = scale
    for d in range(2):
        value_grad = []
        for h in range(8):
            total = gb[h, d, 0, 0:64, :].astype(F32)
            for k in range(1, 4):
                total += gb[h, d, k, 0:64, :].astype(F32)
            value_grad.append(total.astype(BF))
        grad_out[d] = mm_nt(jnp.concatenate(value_grad, axis=1), bdc[...])


def msa_backward(gain, ws, context, tail, normed, scale, partial, out, bds):
    spread(ws[...], False, bds)
    grads = []
    for d in range(2):
        gate_grad = [(tail[h, d] * context[h, d].astype(F32)).astype(BF) for h in range(8)]
        grad = partial[d] + mm_nt(jnp.concatenate(gate_grad, axis=1), bds[...])
        grads += [grad[:, k * 128 : (k + 1) * 128] for k in range(8)]
    ones = averager()
    scaled = jnp.concatenate(grads, axis=0) * twice(gain)
    xhat = normed[...]
    result = scale[...] * (
        scaled - half_means(scaled, ones) - xhat * half_means(scaled * xhat, ones)
    )
    for k in range(16):
        rows = result[k * 64 : (k + 1) * 64]
        out[2 * k] = rows[:, 0:64].astype(BF)
        out[2 * k + 1] = rows[:, 64:128].astype(BF)


def exchange(x, axes):
    return lax.all_to_all(x, axes, 0, 0, tiled=True)


def swap(x, k):
    return lax.ppermute(x, "b", [(i, i ^ k) for i in range(4)])


def shape(dims, dtype):
    return jax.ShapeDtypeStruct(dims, dtype)


def shards(msa, pair, adj, flags, chains, positions, msa_gain, pair_gain, wc, ws, wf, wp, table):
    vm = pl.BlockSpec()
    sm = pl.BlockSpec(memory_space=pltpu.SMEM)
    gp, gq = ("row", "d", "a"), ("row", "d", "b")
    gain = msa_gain.reshape(1, 64)

    u_send, tail = pl.pallas_call(
        msa_updates,
        out_shape=(shape((8, 2, 4, 64, 128), BF), shape((8, 2, 64, 128), F32)),
        in_specs=[sm] + [vm] * 5,
        out_specs=(vm, vm),
        scratch_shapes=[pltpu.VMEM((1024, 1024), BF)] * 2,
        compiler_params=WHOLE,
        name="msa_updates",
    )(flags, msa, adj, gain, ws, wf)
    values = pl.pallas_call(
        msa_values,
        out_shape=shape((8, 2, 64, 128), BF),
        in_specs=[vm] * 3,
        out_specs=vm,
        scratch_shapes=[pltpu.VMEM((1024, 1024), BF)],
        compiler_params=WHOLE,
        name="msa_values",
    )(msa, gain, wc)
    ub = exchange(u_send.reshape(64, 64, 128), gq).reshape(8, 8, 64, 128)

    row = lax.axis_index("row")
    col = lax.axis_index("d") * 16 + lax.axis_index("b") * 4 + lax.axis_index("a")

    def rows_of(x):
        return lax.dynamic_slice_in_dim(x, row * 256, 256).reshape(4, 2, 4, 8).transpose(0, 2, 3, 1)

    def cols_of(x):
        return lax.dynamic_slice_in_dim(x, col * 64, 64)

    offset = jnp.clip(rows_of(positions)[..., None] - cols_of(positions) + RMAX, 0, 2 * RMAX)
    bins = jnp.where(rows_of(chains)[..., None] == cols_of(chains), offset, 2 * RMAX + 1)
    bins = bins.reshape(16, 1, 1024)
    scaled = (wp * pair_gain[:, None]).T
    proj = scaled - jnp.mean(scaled, -1, keepdims=True)
    table_t = jnp.pad(table.T, ((0, 0), (0, 128 - table.shape[0])))

    def const(*dims):
        return pl.BlockSpec(dims, lambda k: (0,) * len(dims))

    vw_send, saved = pl.pallas_call(
        pair_forward,
        grid=(4,),
        out_shape=(shape((8, 2, 4, 112, 128), BF), shape((16, 24, 1024), F32)),
        in_specs=[
            pl.BlockSpec((64, 64, 128), lambda k: (k, 0, 0)),
            pl.BlockSpec((4, 1, 1024), lambda k: (k, 0, 0)),
            const(8, 128),
            const(8, 128),
            const(8, 2, 64, 128),
        ],
        out_specs=(
            pl.BlockSpec((8, 2, 1, 112, 128), lambda k: (0, 0, k, 0, 0)),
            pl.BlockSpec((4, 24, 1024), lambda k: (k, 0, 0)),
        ),
        scratch_shapes=[pltpu.VMEM((8, 32, 128), F32)] * 2,
        compiler_params=VMEM,
        name="pair_forward",
    )(pair, bins, proj, table_t, values)
    vw = exchange(vw_send.reshape(64, 112, 128), gp).reshape(8, 8, 112, 128)

    block = lax.axis_index("b").reshape(1)
    piece = shape((8, 2, 64, 128), BF)
    p_raw, stats, *pieces = pl.pallas_call(
        merge_products,
        out_shape=(shape((8, 2, 2, 16, 512), BF), shape((8, 512), F32)) + (piece,) * 4,
        in_specs=[sm, vm, vm],
        out_specs=(vm,) * 6,
        scratch_shapes=[pltpu.VMEM((8, 2, 2, 16, 128), F32), pltpu.VMEM((8, 512, 128), BF)],
        compiler_params=VMEM,
        name="merge_products",
    )(block, ub, vw)
    shares = [stats] + [swap(stats, k) for k in (1, 2, 3)]
    pieces = pieces[:1] + [swap(pieces[k], k) for k in (1, 2, 3)]
    scores = pl.pallas_call(
        score_products,
        out_shape=shape((512, 512), F32),
        in_specs=[vm, vm],
        out_specs=vm,
        compiler_params=VMEM,
        name="score_products",
    )(ub, vw)
    gd_send = pl.pallas_call(
        gradients,
        out_shape=shape((8, 8, 96, 128), BF),
        in_specs=[vm] * 7 + [pl.BlockSpec(memory_space=pl.ANY)] * 2,
        out_specs=vm,
        compiler_params=VMEM,
        name="gradients",
    )(*shares, p_raw, ub, scores, pieces[1], pieces[3])
    gd = exchange(gd_send.reshape(64, 96, 128), gp).reshape(8, 2, 4, 96, 128)
    context_send = pl.pallas_call(
        context_sum,
        out_shape=piece,
        in_specs=[sm] + [vm] * 8,
        out_specs=vm,
        scratch_shapes=[pltpu.VMEM((512, 8), F32)],
        compiler_params=VMEM,
        name="context_sum",
    )(block, *shares, *pieces)
    context = exchange(context_send.reshape(16, 64, 128), ("row", "d")).reshape(8, 2, 64, 128)
    pair_gradient = pl.pallas_call(
        pair_backward,
        grid=(4,),
        out_shape=shape((256, 64, 128), BF),
        in_specs=[
            pl.BlockSpec((64, 64, 128), lambda k: (k, 0, 0)),
            pl.BlockSpec((8, 2, 1, 32, 128), lambda k: (0, 0, k, 2, 0)),
            pl.BlockSpec((4, 24, 1024), lambda k: (k, 0, 0)),
            const(8, 128),
        ],
        out_specs=pl.BlockSpec((64, 64, 128), lambda k: (k, 0, 0)),
        scratch_shapes=[pltpu.VMEM((8, 32, 128), F32)],
        compiler_params=VMEM,
        name="pair_backward",
    )(pair, gd, saved, proj)
    partial = pl.pallas_call(
        msa_partial,
        out_shape=(shape((1024, 128), F32), shape((1024, 128), F32), shape((2, 64, 1024), F32)),
        in_specs=[vm] * 3,
        out_specs=(vm, vm, vm),
        scratch_shapes=[pltpu.VMEM((1024, 1024), BF)],
        compiler_params=VMEM,
        name="msa_partial",
    )(msa, wc, gd)
    alignment_gradient = pl.pallas_call(
        msa_backward,
        out_shape=shape((32, 64, 64), BF),
        in_specs=[vm] * 7,
        out_specs=vm,
        scratch_shapes=[pltpu.VMEM((1024, 1024), BF)],
        compiler_params=VMEM,
        name="msa_backward",
    )(gain, ws, context, tail, *partial)
    return (alignment_gradient, pair_gradient)


def solution(mesh):
    inner = Mesh(mesh.devices.reshape(8, 2, 4, 4), ("row", "d", "b", "a"))
    res = ("d", "b", "a")
    split = P("row", res, None)
    return jax.shard_map(
        shards,
        mesh=inner,
        in_specs=(split, split, split, P("row")) + (P(),) * 9,
        out_specs=(split, split),
        check_vma=False,
    )
```

```python
import functools

import jax
import jax.numpy as jnp
from jax import lax
from jax.experimental import pallas as pl
from jax.experimental.pallas import tpu as pltpu
from jax.sharding import Mesh
from jax.sharding import PartitionSpec as P

RMAX = 32
EPS = 1e-05
BF = jnp.bfloat16
F32 = jnp.float32
VMEM = pltpu.CompilerParams(vmem_limit_bytes=48 * 1024 * 1024)
WHOLE = pltpu.CompilerParams(vmem_limit_bytes=60 * 1024 * 1024)
HALF = 64


def mm(a, b):
    return lax.dot_general(a, b, (((1,), (0,)), ((), ())), preferred_element_type=F32)


def mm_nt(a, b):
    return lax.dot_general(a, b, (((1,), (1,)), ((), ())), preferred_element_type=F32)


def mm_tn(a, b):
    return lax.dot_general(a, b, (((0,), (0,)), ((), ())), preferred_element_type=F32)


def iota(shape, dim):
    return lax.broadcasted_iota(jnp.int32, shape, dim)


def split3(x):
    hi = x.astype(BF).astype(F32)
    mid = (x - hi).astype(BF).astype(F32)
    return hi, mid, x - hi - mid


def spread(weight, transposed, out_ref):
    k, l = iota((64, 1024), 0), iota((64, 1024), 1)
    pick = jnp.where((k // 8 == l // 128) & (k % 8 == l % 8), 1.0, 0.0).astype(BF)
    wide = mm_tn(weight, pick) if transposed else mm(weight, pick)
    owner = (l % 128) // 8
    for s in range(16):
        out_ref[s * 64 : (s + 1) * 64, :] = jnp.where(owner == s, wide, 0.0).astype(BF)


def averager():
    half = (iota((128, 128), 0) < 64) == (iota((128, 128), 1) < 64)
    return jnp.where(half, 1.0 / 64, 0.0).astype(BF)


def half_means(x, ones):
    hi = x.astype(BF)
    return mm(hi, ones) + mm((x - hi.astype(F32)).astype(BF), ones)


def paired(x):
    return jnp.concatenate([jnp.concatenate([x(2 * k), x(2 * k + 1)], axis=1) for k in range(16)], axis=0)


def beside(x, d):
    return jnp.concatenate([x[(d * 8 + k) * 64 : (d * 8 + k + 1) * 64] for k in range(8)], axis=1)


def standardize(x, ones):
    center = x.astype(F32) - mm(x, ones)
    scale = lax.rsqrt(half_means(center * center, ones) + EPS)
    return center * scale, scale


def twice(gain):
    return jnp.concatenate([gain[...], gain[...]], axis=1)


def msa_forward(flags, msa, adj, gain, wc, ws, wf, u_out, v_out, t_out, bdc, bds, bdf):
    spread(wc[...], False, bdc)
    spread(ws[...], False, bds)
    spread(wf[...], True, bdf)
    normed, _ = standardize(paired(lambda s: msa[s]), averager())
    normed = (normed * twice(gain)).astype(BF)
    masked = paired(lambda s: (adj[s].astype(F32) * flags[s].astype(F32)).astype(BF))
    for d in range(2):
        x = beside(normed, d)
        values = mm(x, bdc[...]).astype(BF)
        gate = jax.nn.sigmoid(mm(x, bds[...]))
        moved = gate * mm(beside(masked, d), bdf[...])
        update = moved.astype(BF)
        tail = moved * (1.0 - gate)
        for h in range(8):
            cols = slice(h * 128, (h + 1) * 128)
            u_out[h, d] = update[:, cols]
            v_out[h, d] = values[:, cols]
            t_out[h, d] = tail[:, cols]


def partner(x, k, lane):
    return jnp.where(lane & k == 0, pltpu.roll(x, 128 - k, 1), pltpu.roll(x, k, 1))


def pair_forward(
    row, col, chain, position, chains, positions, pair, gain, wp, table, v_in, after,
    out, saved, proj, p_s, m_s, w_s,
):
    w_s[...] = jnp.zeros((8, 128), F32)
    w_s[:, 0 : table.shape[1]] = table[...]
    scaled = wp[...] * gain[...]
    scaled = scaled - jnp.mean(scaled, -1, keepdims=True)
    proj[...] = scaled
    w_hi, w_mid, w_lo = split3(scaled)
    ones8 = jnp.full((8, 128), 1.0 / 128, F32)
    lhs = jnp.concatenate([w_hi, w_mid, w_lo, ones8], axis=0).astype(BF)
    ones8 = ones8.astype(BF)
    mean = jnp.full((128, 128), 1.0 / 128, F32).astype(BF)
    b_lhs = jnp.concatenate(list(split3(w_s[...])) + [jnp.zeros((8, 128), F32)], axis=0).astype(BF)
    lane = iota((8, 128), 1)
    klass = iota((128, 1024), 0)
    left = iota((1, 128), 1) < HALF

    def own_columns(ref):
        both = ref[pl.ds(col[0] // 2, 1), :]
        return jnp.where(left == (col[0] % 2 == 0), both, pltpu.roll(both, 64, 1))

    chain_j, position_j = own_columns(chains), own_columns(positions)
    begin = row[0] * 256 + pl.program_id(0) * 64
    for g in range(4):
        x = jnp.concatenate(
            [pair[e * 32 + g * 8 + rho] for rho in range(8) for e in range(2)], axis=0
        )
        center = x.astype(F32) - mm(x, mean)
        square = center * center
        s_hi = square.astype(BF)
        s_lo = (square - s_hi.astype(F32)).astype(BF)
        var = mm_nt(ones8, s_hi) + mm_nt(ones8, s_lo)
        z = mm_nt(lhs, x)
        scale = lax.rsqrt(var + EPS)
        t = (z[0:8] + z[8:16] + z[16:24]) * scale
        saved[g, 0:8, :] = t
        saved[g, 8:16, :] = scale
        saved[g, 16:24, :] = z[24:32]
        bins = []
        for rho in range(8):
            i = begin + g * 8 + rho
            offset = jnp.where(left, position[i], position[i + 32]) - position_j
            near = jnp.clip(offset + RMAX, 0, 2 * RMAX)
            same = jnp.where(left, chain[i], chain[i + 32]) == chain_j
            bins.append(jnp.where(same, near, 2 * RMAX + 1))
        onehot = jnp.where(klass == jnp.concatenate(bins, axis=1), 1.0, 0.0).astype(BF)
        zb = mm(b_lhs, onehot)
        logits = t + (zb[0:8] + zb[8:16] + zb[16:24])
        for rho in range(8):
            part = logits[:, rho * 128 : (rho + 1) * 128]
            top = part
            for k in (1, 2, 4, 8, 16, 32):
                top = jnp.maximum(top, partner(top, k, lane))
            top = top.astype(BF).astype(F32)
            p_s[:, g * 8 + rho, :] = jnp.exp(part - top)
            m_s[:, g * 8 + rho, :] = top
    quarter = iota((16, 128), 1) // 32
    for h in range(8):
        weights = p_s[h].astype(BF)
        low, high = m_s[h, 0:16, :], m_s[h, 16:32, :]
        packed = jnp.where(
            quarter == 0,
            low,
            jnp.where(
                quarter == 1, pltpu.roll(low, 64, 1), jnp.where(quarter == 2, pltpu.roll(high, 64, 1), high)
            ),
        ).astype(BF)
        for d in range(2):
            out[h, d, 0, 0:64, :] = v_in[h, d]
            out[h, d, 0, 64:96, :] = weights
            out[h, d, 0, 96:112, :] = packed


def rows_at(d, block):
    return pl.ds(pl.multiple_of(d * 256 + block * 64, 64), 64)


def gather_updates(block, mine, first, second_a, second_b, third, out):
    for r in range(8):
        second = second_a.at[r] if r < 4 else second_b.at[r - 4]
        for d in range(2):
            for k, x in enumerate((mine.at[r], first.at[r], second, third.at[r])):
                out[r, rows_at(d, block[0] ^ k), :] = x[d]


def merge_products(block, ub, vw, p_out, stats, own, first, third, m_s, c_s):
    lane = iota((128, 128), 1)
    quarter = lane // 32
    left = lane < HALF
    for half in range(2):
        tops = []
        for c in range(8):
            q = vw[:, c, 96:112, :].astype(F32).reshape(128, 128)
            q64 = pltpu.roll(q, 64, 1)
            if half == 0:
                tops.append(jnp.where(quarter == 0, q, jnp.where(quarter == 3, q64, pltpu.roll(q, 32, 1))))
            else:
                tops.append(jnp.where(quarter == 0, q64, jnp.where(quarter == 3, q, pltpu.roll(q, 96, 1))))
        peak = functools.reduce(jnp.maximum, tops)
        crossed = pltpu.roll(peak, 64, 1)
        m_s[:, 0, half] = jnp.where(left, peak, crossed).reshape(8, 16, 128)
        m_s[:, 1, half] = jnp.where(left, crossed, peak).reshape(8, 16, 128)
        rows = slice(64 + half * 16, 80 + half * 16)
        for cp in range(4):
            one, two = [
                vw[:, c, rows, :].astype(F32).reshape(128, 128) * jnp.exp(tops[c] - peak)
                for c in (2 * cp, 2 * cp + 1)
            ]
            cols = slice(cp * 128, (cp + 1) * 128)
            even = jnp.where(left, one, pltpu.roll(two, 64, 1)).astype(BF)
            odd = jnp.where(left, pltpu.roll(one, 64, 1), two).astype(BF)
            p_out[:, 0, half, :, cols] = even.reshape(8, 16, 128)
            p_out[:, 1, half, :, cols] = odd.reshape(8, 16, 128)
    p = p_out[...].reshape(512, 512)
    total = mm(p, jnp.full((512, 128), 1.0, F32).astype(BF))
    acc = jnp.zeros((512, 128), F32)
    for r in range(0, 8, 2):
        v = jnp.concatenate([vw[r + k, :, 0:64, :].reshape(512, 128) for k in range(2)], axis=1)
        c = mm(p, v)
        for k in range(2):
            part = c[:, k * 128 : (k + 1) * 128]
            acc += ub[r + k].reshape(512, 128).astype(F32) * part
            c_s[r + k] = part.astype(BF)
    score = jnp.sum(acc, axis=1, keepdims=True)
    column = iota((512, 128), 1)
    mixed = m_s[...].reshape(512, 128)
    for at, value in enumerate(split3(total)[:2] + split3(jnp.broadcast_to(score, (512, 128)))):
        mixed = jnp.where(column == at + 1, value, mixed)
    rows = jnp.transpose(mixed)[0:8]
    rows = jnp.concatenate([rows[:, q * 128 : (q + 1) * 128] for q in range(4)], axis=0).astype(BF)
    stats[...] = rows
    first[1024:1056, :] = rows
    third[1024:1056, :] = rows
    for d in range(2):
        for r in range(8):
            zero, one, two, three = [c_s[r, rows_at(d, block[0] ^ k), :] for k in range(4)]
            own[0, r, d] = zero
            at = ((r % 4) * 2 + d) * 64
            out, direct, passed = (first, one, two) if r < 4 else (third, three, two)
            own[1, r, d] = three if r < 4 else one
            out[at : at + 64, :] = direct
            out[512 + at : 576 + at, :] = passed


def score_products(msa, ub, vw, out, normed_out, scale_out):
    acc = jnp.zeros((512, 512), F32)
    for r in range(0, 8, 2):
        u = jnp.concatenate([ub[r + k].reshape(512, 128) for k in range(2)], axis=1)
        v = jnp.concatenate([vw[r + k, :, 0:64, :].reshape(512, 128) for k in range(2)], axis=1)
        acc += mm_nt(u, v)
    out[...] = acc
    normed_out[...], scale_out[...] = standardize(paired(lambda s: msa[s]), averager())


def streamed(stats):
    rows = []
    for ref in stats:
        x = ref[-32:, :].astype(F32)
        rows.append(jnp.concatenate([x[q * 8 : q * 8 + 8] for q in range(4)], axis=1))
    peak = functools.reduce(jnp.maximum, [x[0:1] for x in rows])
    factor = [jnp.exp(x[0:1] - peak) for x in rows]
    total = sum(f * (x[1:2] + x[2:3]) for f, x in zip(factor, rows))
    return [f / total for f in factor], [x[3:4] + x[4:5] + x[5:6] for x in rows]


def gradients(own, first, second, third, p_in, ub, scores, out):
    share, rows = streamed((own, first, second, third))
    row_total = sum(f * x for f, x in zip(share, rows))
    which = iota((8, 512), 0)
    columns = jnp.transpose(jnp.where(which == 0, share[0], jnp.where(which == 1, row_total, 0.0)))
    p = (p_in[...].reshape(512, 512).astype(F32) * columns[:, 0:1]).astype(BF)
    grad = (p.astype(F32) * (scores[...] - columns[:, 1:2])).reshape(8, 2, 32, 512)
    left = iota((256, 128), 1) < HALF
    for cp in range(4):
        cols = slice(cp * 128, (cp + 1) * 128)
        even, odd = [grad[:, e, :, cols].reshape(256, 128) for e in range(2)]
        one = jnp.where(left, even, pltpu.roll(odd, 64, 1)).astype(BF)
        two = jnp.where(left, pltpu.roll(even, 64, 1), odd).astype(BF)
        out[:, 2 * cp, 64:96, :] = one.reshape(8, 32, 128)
        out[:, 2 * cp + 1, 64:96, :] = two.reshape(8, 32, 128)
    pt = jnp.transpose(p)
    for r in range(0, 8, 2):
        u = jnp.concatenate([ub[r + k].reshape(512, 128) for k in range(2)], axis=1)
        grad_v = mm(pt, u).astype(BF)
        for k in range(2):
            out[r + k, :, 0:64, :] = grad_v[:, k * 128 : (k + 1) * 128].reshape(8, 64, 128)


def share_columns(stats, f_s):
    share, _ = streamed(stats)
    which = iota((8, 512), 0)
    mixed = jnp.zeros((8, 512), F32)
    for k in range(4):
        mixed = jnp.where(which == k, share[k], mixed)
    f_s[...] = jnp.transpose(mixed)


def context_on_the_way(block, s0, s2, c, first, third, to_third, to_first, f_s):
    share_columns((s0, first, s2, third), f_s)
    for d in range(2):
        f_3, f_1 = f_s[rows_at(d, block[0] ^ 3), :], f_s[rows_at(d, block[0] ^ 1), :]
        for r in range(4):
            at = (r * 2 + d) * 64
            to_third[r, d] = (
                c[1, r, d].astype(F32) * f_3[:, 0:1] + first[512 + at : 576 + at, :].astype(F32) * f_3[:, 1:2]
            ).astype(BF)
            to_first[r, d] = (
                c[1, r + 4, d].astype(F32) * f_1[:, 0:1] + third[512 + at : 576 + at, :].astype(F32) * f_1[:, 3:4]
            ).astype(BF)


def context_sum(block, s0, s2, c, first, third, from_third, from_first, out, f_s):
    share_columns((s0, first, s2, third), f_s)
    for d in range(2):
        f = f_s[rows_at(d, block[0]), :]
        for r in range(8):
            rows = slice(((r % 4) * 2 + d) * 64, ((r % 4) * 2 + d + 1) * 64)
            near, at, far = (
                (first[rows, :], 1, from_third[r, d]) if r < 4 else (third[rows, :], 3, from_first[r - 4, d])
            )
            out[r, d] = (
                c[0, r, d].astype(F32) * f[:, 0:1] + near.astype(F32) * f[:, at : at + 1] + far.astype(F32)
            ).astype(BF)


def pair_backward(pair, grads, saved, proj, out, g_s):
    w_hi, w_mid, _ = split3(proj[...])
    row = iota((8, 128), 0)
    flag = jnp.where(row < 3, 1.0, 0.0)
    rhs = jnp.concatenate([w_hi, w_hi, w_mid, flag], axis=0).astype(BF)
    rhs_a = jnp.concatenate([flag, jnp.zeros((8, 128), F32)], axis=0).astype(BF)
    g_s[...] = grads[:, 0, 0].astype(F32) + grads[:, 1, 0].astype(F32)
    which = iota((8, 1024), 0)

    def stacked(x):
        hi, mid, low = split3(x)
        return jnp.where(which == 0, hi, jnp.where(which == 1, mid, jnp.where(which == 2, low, 0.0)))

    for g in range(4):
        grad = jnp.concatenate([g_s[:, g * 8 + rho, :] for rho in range(8)], axis=1)
        t, scale, mean = saved[g, 0:8, :], saved[g, 8:16, :], saved[g, 16:24, :]
        slope = jnp.sum(grad * t, axis=0, keepdims=True) * (1.0 / 128)
        alpha = scale * scale * slope
        scaled = grad * scale
        hi = scaled.astype(BF).astype(F32)
        lhs = jnp.concatenate([hi, scaled - hi, hi, stacked(alpha * mean)], axis=0).astype(BF)
        lhs_a = jnp.concatenate([stacked(alpha), jnp.zeros((8, 1024), F32)], axis=0).astype(BF)
        base = mm_tn(lhs, rhs)
        steep = mm_tn(lhs_a, rhs_a)
        for rho in range(8):
            for e in range(2):
                i = e * 32 + g * 8 + rho
                rows = slice((rho * 2 + e) * 64, (rho * 2 + e + 1) * 64)
                out[i] = (base[rows] - steep[rows] * pair[i].astype(F32)).astype(BF)


def msa_partial(wc, gb, grad_out, bdc):
    spread(wc[...], False, bdc)
    for d in range(2):
        value_grad = []
        for h in range(8):
            total = gb[h, d, 0, 0:64, :].astype(F32)
            for k in range(1, 4):
                total += gb[h, d, k, 0:64, :].astype(F32)
            value_grad.append(total.astype(BF))
        grad_out[d] = mm_nt(jnp.concatenate(value_grad, axis=1), bdc[...])


def msa_backward(gain, ws, context, tail, normed, scale, partial, out, bds):
    spread(ws[...], False, bds)
    grads = []
    for d in range(2):
        gate_grad = [(tail[h, d] * context[h, d].astype(F32)).astype(BF) for h in range(8)]
        grad = partial[d] + mm_nt(jnp.concatenate(gate_grad, axis=1), bds[...])
        grads += [grad[:, k * 128 : (k + 1) * 128] for k in range(8)]
    ones = averager()
    scaled = jnp.concatenate(grads, axis=0) * twice(gain)
    xhat = normed[...]
    result = scale[...] * (
        scaled - half_means(scaled, ones) - xhat * half_means(scaled * xhat, ones)
    )
    for k in range(16):
        rows = result[k * 64 : (k + 1) * 64]
        out[2 * k] = rows[:, 0:64].astype(BF)
        out[2 * k + 1] = rows[:, 64:128].astype(BF)


def exchange(x, axes):
    return lax.all_to_all(x, axes, 0, 0, tiled=True)


def swap(x, k):
    return lax.ppermute(x, "b", [(i, i ^ k) for i in range(4)])


def shape(dims, dtype):
    return jax.ShapeDtypeStruct(dims, dtype)


def shards(msa, pair, adj, flags, chains, positions, msa_gain, pair_gain, wc, ws, wf, wp, table):
    vm = pl.BlockSpec()
    sm = pl.BlockSpec(memory_space=pltpu.SMEM)
    gp, rd = ("row", "d", "a"), ("row", "d")
    gain = msa_gain.reshape(1, 64)
    block = lax.axis_index("b").reshape(1)
    piece = shape((8, 2, 64, 128), BF)

    u_send, values, tail = pl.pallas_call(
        msa_forward,
        out_shape=(piece, piece, shape((8, 2, 64, 128), F32)),
        in_specs=[sm] + [vm] * 6,
        out_specs=(vm, vm, vm),
        scratch_shapes=[pltpu.VMEM((1024, 1024), BF)] * 3,
        compiler_params=WHOLE,
        name="msa_forward",
    )(flags, msa, adj, gain, wc, ws, wf)
    mine = exchange(u_send.reshape(16, 64, 128), rd).reshape(8, 2, 64, 128)
    first, third = swap(mine, 1), swap(mine, 3)
    second = swap(first[:4], 3), swap(third[4:], 1)
    ub = pl.pallas_call(
        gather_updates,
        out_shape=shape((8, 512, 128), BF),
        in_specs=[sm] + [vm] * 5,
        out_specs=vm,
        compiler_params=VMEM,
        name="gather_updates",
    )(block, mine, first, *second, third)

    col = lax.axis_index("d") * 16 + lax.axis_index("b") * 4 + lax.axis_index("a")
    def const(*dims):
        return pl.BlockSpec(dims, lambda k: (0,) * len(dims))

    anywhere = pl.BlockSpec(memory_space=pl.ANY)
    vw_send, saved, proj = pl.pallas_call(
        pair_forward,
        grid=(4,),
        out_shape=(shape((8, 2, 4, 112, 128), BF), shape((16, 24, 1024), F32), shape((8, 128), F32)),
        in_specs=[
            sm,
            sm,
            sm,
            sm,
            const(16, 128),
            const(16, 128),
            pl.BlockSpec((64, 64, 128), lambda k: (k, 0, 0)),
            const(1, 128),
            const(8, 128),
            const(8, table.shape[0]),
            const(8, 2, 64, 128),
            anywhere,
        ],
        out_specs=(
            pl.BlockSpec((8, 2, 1, 112, 128), lambda k: (0, 0, k, 0, 0)),
            pl.BlockSpec((4, 24, 1024), lambda k: (k, 0, 0)),
            const(8, 128),
        ),
        scratch_shapes=[pltpu.VMEM((8, 32, 128), F32)] * 2 + [pltpu.VMEM((8, 128), F32)],
        compiler_params=WHOLE,
        name="pair_forward",
    )(
        lax.axis_index("row").reshape(1),
        col.reshape(1),
        chains,
        positions,
        chains.reshape(16, 128),
        positions.reshape(16, 128),
        pair,
        pair_gain.reshape(1, 128),
        wp.T,
        table.T,
        values,
        mine,
    )
    vw_send = pl.pallas_call(
        lambda *refs: None,
        out_shape=shape((8, 2, 4, 112, 128), BF),
        in_specs=[anywhere] * 3,
        out_specs=anywhere,
        input_output_aliases={0: 0},
        compiler_params=WHOLE,
        name="in_order",
    )(vw_send, first, third)
    vw = exchange(vw_send.reshape(64, 112, 128), gp).reshape(8, 8, 112, 128)

    halves = shape((1056, 128), BF)
    p_raw, stats, own, first, third = pl.pallas_call(
        merge_products,
        out_shape=(shape((8, 2, 2, 16, 512), BF), shape((32, 128), BF), shape((2, 8, 2, 64, 128), BF), halves, halves),
        in_specs=[sm, vm, vm],
        out_specs=(vm,) * 5,
        scratch_shapes=[pltpu.VMEM((8, 2, 2, 16, 128), F32), pltpu.VMEM((8, 512, 128), BF)],
        compiler_params=VMEM,
        name="merge_products",
    )(block, ub, vw)
    far, first, third = swap(stats, 2), swap(first, 1), swap(third, 3)
    scores, normed, scale = pl.pallas_call(
        score_products,
        out_shape=(shape((512, 512), F32), shape((1024, 128), F32), shape((1024, 128), F32)),
        in_specs=[vm] * 3,
        out_specs=(vm,) * 3,
        compiler_params=VMEM,
        name="score_products",
    )(msa, ub, vw)
    gd_send = pl.pallas_call(
        gradients,
        out_shape=shape((8, 8, 96, 128), BF),
        in_specs=[vm] * 7,
        out_specs=vm,
        compiler_params=VMEM,
        name="gradients",
    )(stats, first, far, third, p_raw, ub, scores)
    gd = exchange(gd_send.reshape(64, 96, 128), gp).reshape(8, 2, 4, 96, 128)
    half = shape((4, 2, 64, 128), BF)
    to_third, to_first = pl.pallas_call(
        context_on_the_way,
        out_shape=(half, half),
        in_specs=[sm] + [vm] * 5,
        out_specs=(vm, vm),
        scratch_shapes=[pltpu.VMEM((512, 8), F32)],
        compiler_params=WHOLE,
        name="context_on_the_way",
    )(block, stats, far, own, first, third)
    context_send = pl.pallas_call(
        context_sum,
        out_shape=piece,
        in_specs=[sm] + [vm] * 7,
        out_specs=vm,
        scratch_shapes=[pltpu.VMEM((512, 8), F32)],
        compiler_params=WHOLE,
        name="context_sum",
    )(block, stats, far, own, first, third, swap(to_third, 3), swap(to_first, 1))
    context = exchange(context_send.reshape(16, 64, 128), rd).reshape(8, 2, 64, 128)
    pair_gradient = pl.pallas_call(
        pair_backward,
        grid=(4,),
        out_shape=shape((256, 64, 128), BF),
        in_specs=[
            pl.BlockSpec((64, 64, 128), lambda k: (k, 0, 0)),
            pl.BlockSpec((8, 2, 1, 32, 128), lambda k: (0, 0, k, 2, 0)),
            pl.BlockSpec((4, 24, 1024), lambda k: (k, 0, 0)),
            const(8, 128),
        ],
        out_specs=pl.BlockSpec((64, 64, 128), lambda k: (k, 0, 0)),
        scratch_shapes=[pltpu.VMEM((8, 32, 128), F32)],
        compiler_params=VMEM,
        name="pair_backward",
    )(pair, gd, saved, proj)
    partial = pl.pallas_call(
        msa_partial,
        out_shape=shape((2, 64, 1024), F32),
        in_specs=[vm] * 2,
        out_specs=vm,
        scratch_shapes=[pltpu.VMEM((1024, 1024), BF)],
        compiler_params=VMEM,
        name="msa_partial",
    )(wc, gd)
    alignment_gradient = pl.pallas_call(
        msa_backward,
        out_shape=shape((32, 64, 64), BF),
        in_specs=[vm] * 7,
        out_specs=vm,
        scratch_shapes=[pltpu.VMEM((1024, 1024), BF)],
        compiler_params=WHOLE,
        name="msa_backward",
    )(gain, ws, context, tail, normed, scale, partial)
    return (alignment_gradient, pair_gradient)


def solution(mesh):
    inner = Mesh(mesh.devices.reshape(8, 2, 4, 4), ("row", "d", "b", "a"))
    res = ("d", "b", "a")
    split = P("row", res, None)
    return jax.shard_map(
        shards,
        mesh=inner,
        in_specs=(split, split, split, P("row")) + (P(),) * 9,
        out_specs=(split, split),
        check_vma=False,
    )
```

```python
import functools

import jax
import jax.numpy as jnp
from jax import lax
from jax.experimental import pallas as pl
from jax.experimental.pallas import tpu as pltpu
from jax.sharding import Mesh
from jax.sharding import PartitionSpec as P

RMAX = 32
EPS = 1e-05
BF = jnp.bfloat16
F32 = jnp.float32
VMEM = pltpu.CompilerParams(vmem_limit_bytes=48 * 1024 * 1024)
WHOLE = pltpu.CompilerParams(vmem_limit_bytes=60 * 1024 * 1024)
HALF = 64


def mm(a, b):
    return lax.dot_general(a, b, (((1,), (0,)), ((), ())), preferred_element_type=F32)


def mm_nt(a, b):
    return lax.dot_general(a, b, (((1,), (1,)), ((), ())), preferred_element_type=F32)


def mm_tn(a, b):
    return lax.dot_general(a, b, (((0,), (0,)), ((), ())), preferred_element_type=F32)


def iota(shape, dim):
    return lax.broadcasted_iota(jnp.int32, shape, dim)


def split3(x):
    hi = x.astype(BF).astype(F32)
    mid = (x - hi).astype(BF).astype(F32)
    return hi, mid, x - hi - mid


def spread(weight, transposed, out_ref):
    k, l = iota((64, 1024), 0), iota((64, 1024), 1)
    pick = jnp.where((k // 8 == l // 128) & (k % 8 == l % 8), 1.0, 0.0).astype(BF)
    wide = mm_tn(weight, pick) if transposed else mm(weight, pick)
    owner = (l % 128) // 8
    for s in range(16):
        out_ref[s * 64 : (s + 1) * 64, :] = jnp.where(owner == s, wide, 0.0).astype(BF)


def averager():
    half = (iota((128, 128), 0) < 64) == (iota((128, 128), 1) < 64)
    return jnp.where(half, 1.0 / 64, 0.0).astype(BF)


def half_means(x, ones):
    hi = x.astype(BF)
    return mm(hi, ones) + mm((x - hi.astype(F32)).astype(BF), ones)


def paired(x):
    return jnp.concatenate([jnp.concatenate([x(2 * k), x(2 * k + 1)], axis=1) for k in range(16)], axis=0)


def beside(x, d):
    return jnp.concatenate([x[(d * 8 + k) * 64 : (d * 8 + k + 1) * 64] for k in range(8)], axis=1)


def standardize(x, ones):
    center = x.astype(F32) - mm(x, ones)
    scale = lax.rsqrt(half_means(center * center, ones) + EPS)
    return center * scale, scale


def twice(gain):
    return jnp.concatenate([gain[...], gain[...]], axis=1)


def msa_forward(flags, msa, adj, gain, wc, ws, wf, u_out, v_out, t_out, bdc, bds, bdf):
    spread(wc[...], False, bdc)
    spread(ws[...], False, bds)
    spread(wf[...], True, bdf)
    normed, _ = standardize(paired(lambda s: msa[s]), averager())
    normed = (normed * twice(gain)).astype(BF)
    masked = paired(lambda s: (adj[s].astype(F32) * flags[s].astype(F32)).astype(BF))
    for d in range(2):
        x = beside(normed, d)
        values = mm(x, bdc[...]).astype(BF)
        gate = jax.nn.sigmoid(mm(x, bds[...]))
        moved = gate * mm(beside(masked, d), bdf[...])
        update = moved.astype(BF)
        tail = moved * (1.0 - gate)
        for h in range(8):
            cols = slice(h * 128, (h + 1) * 128)
            u_out[h, d] = update[:, cols]
            v_out[h, d] = values[:, cols]
            t_out[h, d] = tail[:, cols]


def partner(x, k, lane):
    return jnp.where(lane & k == 0, pltpu.roll(x, 128 - k, 1), pltpu.roll(x, k, 1))


def pair_forward(
    row, col, chain, position, chains, positions, pair, gain, wp, table, v_in, after,
    out, saved, proj, p_s, m_s, w_s,
):
    w_s[...] = jnp.zeros((8, 128), F32)
    w_s[:, 0 : table.shape[1]] = table[...]
    scaled = wp[...] * gain[...]
    scaled = scaled - jnp.mean(scaled, -1, keepdims=True)
    proj[...] = scaled
    w_hi, w_mid, w_lo = split3(scaled)
    ones8 = jnp.full((8, 128), 1.0 / 128, F32)
    lhs = jnp.concatenate([w_hi, w_mid, w_lo, ones8], axis=0).astype(BF)
    ones8 = ones8.astype(BF)
    mean = jnp.full((128, 128), 1.0 / 128, F32).astype(BF)
    b_lhs = jnp.concatenate(list(split3(w_s[...])) + [jnp.zeros((8, 128), F32)], axis=0).astype(BF)
    lane = iota((8, 128), 1)
    klass = iota((128, 1024), 0)
    left = iota((1, 128), 1) < HALF

    def own_columns(ref):
        both = ref[pl.ds(col[0] // 2, 1), :]
        return jnp.where(left == (col[0] % 2 == 0), both, pltpu.roll(both, 64, 1))

    chain_j, position_j = own_columns(chains), own_columns(positions)
    begin = row[0] * 256 + pl.program_id(0) * 64
    for g in range(4):
        x = jnp.concatenate(
            [pair[e * 32 + g * 8 + rho] for rho in range(8) for e in range(2)], axis=0
        )
        center = x.astype(F32) - mm(x, mean)
        square = center * center
        s_hi = square.astype(BF)
        s_lo = (square - s_hi.astype(F32)).astype(BF)
        var = mm_nt(ones8, s_hi) + mm_nt(ones8, s_lo)
        z = mm_nt(lhs, x)
        scale = lax.rsqrt(var + EPS)
        t = (z[0:8] + z[8:16] + z[16:24]) * scale
        saved[g, 0:8, :] = t
        saved[g, 8:16, :] = scale
        saved[g, 16:24, :] = z[24:32]
        bins = []
        for rho in range(8):
            i = begin + g * 8 + rho
            offset = jnp.where(left, position[i], position[i + 32]) - position_j
            near = jnp.clip(offset + RMAX, 0, 2 * RMAX)
            same = jnp.where(left, chain[i], chain[i + 32]) == chain_j
            bins.append(jnp.where(same, near, 2 * RMAX + 1))
        onehot = jnp.where(klass == jnp.concatenate(bins, axis=1), 1.0, 0.0).astype(BF)
        zb = mm(b_lhs, onehot)
        logits = t + (zb[0:8] + zb[8:16] + zb[16:24])
        for rho in range(8):
            part = logits[:, rho * 128 : (rho + 1) * 128]
            top = part
            for k in (1, 2, 4, 8, 16, 32):
                top = jnp.maximum(top, partner(top, k, lane))
            top = top.astype(BF).astype(F32)
            p_s[:, g * 8 + rho, :] = jnp.exp(part - top)
            m_s[:, g * 8 + rho, :] = top
    quarter = iota((16, 128), 1) // 32
    for h in range(8):
        weights = p_s[h].astype(BF)
        low, high = m_s[h, 0:16, :], m_s[h, 16:32, :]
        packed = jnp.where(
            quarter == 0,
            low,
            jnp.where(
                quarter == 1, pltpu.roll(low, 64, 1), jnp.where(quarter == 2, pltpu.roll(high, 64, 1), high)
            ),
        ).astype(BF)
        for d in range(2):
            out[h, d, 0, 0:64, :] = v_in[h, d]
            out[h, d, 0, 64:96, :] = weights
            out[h, d, 0, 96:112, :] = packed


def rows_at(d, block):
    return pl.ds(pl.multiple_of(d * 256 + block * 64, 64), 64)


def gather_updates(block, mine, first, second_a, second_b, third, out):
    for r in range(8):
        second = second_a.at[r] if r < 4 else second_b.at[r - 4]
        for d in range(2):
            for k, x in enumerate((mine.at[r], first.at[r], second, third.at[r])):
                out[r, rows_at(d, block[0] ^ k), :] = x[d]


def merge_products(block, ub, vw, p_out, stats, own, first, third, m_s, c_s):
    lane = iota((128, 128), 1)
    quarter = lane // 32
    left = lane < HALF
    for half in range(2):
        tops = []
        for c in range(8):
            q = vw[:, c, 96:112, :].astype(F32).reshape(128, 128)
            q64 = pltpu.roll(q, 64, 1)
            if half == 0:
                tops.append(jnp.where(quarter == 0, q, jnp.where(quarter == 3, q64, pltpu.roll(q, 32, 1))))
            else:
                tops.append(jnp.where(quarter == 0, q64, jnp.where(quarter == 3, q, pltpu.roll(q, 96, 1))))
        peak = functools.reduce(jnp.maximum, tops)
        crossed = pltpu.roll(peak, 64, 1)
        m_s[:, 0, half] = jnp.where(left, peak, crossed).reshape(8, 16, 128)
        m_s[:, 1, half] = jnp.where(left, crossed, peak).reshape(8, 16, 128)
        rows = slice(64 + half * 16, 80 + half * 16)
        for cp in range(4):
            one, two = [
                vw[:, c, rows, :].astype(F32).reshape(128, 128) * jnp.exp(tops[c] - peak)
                for c in (2 * cp, 2 * cp + 1)
            ]
            cols = slice(cp * 128, (cp + 1) * 128)
            even = jnp.where(left, one, pltpu.roll(two, 64, 1)).astype(BF)
            odd = jnp.where(left, pltpu.roll(one, 64, 1), two).astype(BF)
            p_out[:, 0, half, :, cols] = even.reshape(8, 16, 128)
            p_out[:, 1, half, :, cols] = odd.reshape(8, 16, 128)
    p = p_out[...].reshape(512, 512)
    total = mm(p, jnp.full((512, 128), 1.0, F32).astype(BF))
    acc = jnp.zeros((512, 128), F32)
    for r in range(0, 8, 2):
        v = jnp.concatenate([vw[r + k, :, 0:64, :].reshape(512, 128) for k in range(2)], axis=1)
        c = mm(p, v)
        for k in range(2):
            part = c[:, k * 128 : (k + 1) * 128]
            acc += ub[r + k].reshape(512, 128).astype(F32) * part
            c_s[r + k] = part.astype(BF)
    score = jnp.sum(acc, axis=1, keepdims=True)
    column = iota((512, 128), 1)
    mixed = m_s[...].reshape(512, 128)
    for at, value in enumerate(split3(total)[:2] + split3(jnp.broadcast_to(score, (512, 128)))):
        mixed = jnp.where(column == at + 1, value, mixed)
    rows = jnp.transpose(mixed)[0:8]
    rows = jnp.concatenate([rows[:, q * 128 : (q + 1) * 128] for q in range(4)], axis=0).astype(BF)
    stats[...] = rows
    first[1024:1056, :] = rows
    third[1024:1056, :] = rows
    for d in range(2):
        for r in range(8):
            zero, one, two, three = [c_s[r, rows_at(d, block[0] ^ k), :] for k in range(4)]
            own[0, r, d] = zero
            at = ((r % 4) * 2 + d) * 64
            out, direct, passed = (first, one, two) if r < 4 else (third, three, two)
            own[1, r, d] = three if r < 4 else one
            out[at : at + 64, :] = direct
            out[512 + at : 576 + at, :] = passed


def score_products(msa, ub, vw, out, normed_out, scale_out):
    acc = jnp.zeros((512, 512), F32)
    for r in range(0, 8, 2):
        u = jnp.concatenate([ub[r + k].reshape(512, 128) for k in range(2)], axis=1)
        v = jnp.concatenate([vw[r + k, :, 0:64, :].reshape(512, 128) for k in range(2)], axis=1)
        acc += mm_nt(u, v)
    out[...] = acc
    normed_out[...], scale_out[...] = standardize(paired(lambda s: msa[s]), averager())


def streamed(stats):
    rows = []
    for ref in stats:
        x = ref[-32:, :].astype(F32)
        rows.append(jnp.concatenate([x[q * 8 : q * 8 + 8] for q in range(4)], axis=1))
    peak = functools.reduce(jnp.maximum, [x[0:1] for x in rows])
    factor = [jnp.exp(x[0:1] - peak) for x in rows]
    total = sum(f * (x[1:2] + x[2:3]) for f, x in zip(factor, rows))
    return [f / total for f in factor], [x[3:4] + x[4:5] + x[5:6] for x in rows]


def gradients(own, first, second, third, p_in, ub, scores, out):
    share, rows = streamed((own, first, second, third))
    row_total = sum(f * x for f, x in zip(share, rows))
    which = iota((8, 512), 0)
    columns = jnp.transpose(jnp.where(which == 0, share[0], jnp.where(which == 1, row_total, 0.0)))
    p = (p_in[...].reshape(512, 512).astype(F32) * columns[:, 0:1]).astype(BF)
    grad = (p.astype(F32) * (scores[...] - columns[:, 1:2])).reshape(8, 2, 32, 512)
    left = iota((256, 128), 1) < HALF
    for cp in range(4):
        cols = slice(cp * 128, (cp + 1) * 128)
        even, odd = [grad[:, e, :, cols].reshape(256, 128) for e in range(2)]
        one = jnp.where(left, even, pltpu.roll(odd, 64, 1)).astype(BF)
        two = jnp.where(left, pltpu.roll(even, 64, 1), odd).astype(BF)
        out[:, 2 * cp, 64:96, :] = one.reshape(8, 32, 128)
        out[:, 2 * cp + 1, 64:96, :] = two.reshape(8, 32, 128)
    pt = jnp.transpose(p)
    for r in range(0, 8, 2):
        u = jnp.concatenate([ub[r + k].reshape(512, 128) for k in range(2)], axis=1)
        grad_v = mm(pt, u).astype(BF)
        for k in range(2):
            out[r + k, :, 0:64, :] = grad_v[:, k * 128 : (k + 1) * 128].reshape(8, 64, 128)


def share_columns(stats, f_s):
    share, _ = streamed(stats)
    which = iota((8, 512), 0)
    mixed = jnp.zeros((8, 512), F32)
    for k in range(4):
        mixed = jnp.where(which == k, share[k], mixed)
    f_s[...] = jnp.transpose(mixed)


def context_on_the_way(block, s0, s2, c, first, third, to_third, to_first, base, f_s):
    share_columns((s0, first, s2, third), f_s)
    for d in range(2):
        f_0, f_1, f_3 = [f_s[rows_at(d, block[0] ^ k), :] for k in (0, 1, 3)]
        for r in range(4):
            at = (r * 2 + d) * 64
            near, far = slice(at, at + 64), slice(512 + at, 576 + at)
            to_third[r, d] = (
                c[1, r, d].astype(F32) * f_3[:, 0:1] + first[far, :].astype(F32) * f_3[:, 1:2]
            ).astype(BF)
            to_first[r, d] = (
                c[1, r + 4, d].astype(F32) * f_1[:, 0:1] + third[far, :].astype(F32) * f_1[:, 3:4]
            ).astype(BF)
            base[r, d] = c[0, r, d].astype(F32) * f_0[:, 0:1] + first[near, :].astype(F32) * f_0[:, 1:2]
            base[r + 4, d] = (
                c[0, r + 4, d].astype(F32) * f_0[:, 0:1] + third[near, :].astype(F32) * f_0[:, 3:4]
            )


def context_sum(base, from_third, from_first, out):
    out[0:4] = (base[0:4] + from_third[...].astype(F32)).astype(BF)
    out[4:8] = (base[4:8] + from_first[...].astype(F32)).astype(BF)


def pair_backward(pair, grads, saved, proj, out, g_s):
    w_hi, w_mid, _ = split3(proj[...])
    row = iota((8, 128), 0)
    flag = jnp.where(row < 3, 1.0, 0.0)
    rhs = jnp.concatenate([w_hi, w_hi, w_mid, flag], axis=0).astype(BF)
    rhs_a = jnp.concatenate([flag, jnp.zeros((8, 128), F32)], axis=0).astype(BF)
    g_s[...] = grads[:, 0, 0].astype(F32) + grads[:, 1, 0].astype(F32)
    which = iota((8, 1024), 0)

    def stacked(x):
        hi, mid, low = split3(x)
        return jnp.where(which == 0, hi, jnp.where(which == 1, mid, jnp.where(which == 2, low, 0.0)))

    for g in range(4):
        grad = jnp.concatenate([g_s[:, g * 8 + rho, :] for rho in range(8)], axis=1)
        t, scale, mean = saved[g, 0:8, :], saved[g, 8:16, :], saved[g, 16:24, :]
        slope = jnp.sum(grad * t, axis=0, keepdims=True) * (1.0 / 128)
        alpha = scale * scale * slope
        scaled = grad * scale
        hi = scaled.astype(BF).astype(F32)
        lhs = jnp.concatenate([hi, scaled - hi, hi, stacked(alpha * mean)], axis=0).astype(BF)
        lhs_a = jnp.concatenate([stacked(alpha), jnp.zeros((8, 1024), F32)], axis=0).astype(BF)
        base = mm_tn(lhs, rhs)
        steep = mm_tn(lhs_a, rhs_a)
        for rho in range(8):
            for e in range(2):
                i = e * 32 + g * 8 + rho
                rows = slice((rho * 2 + e) * 64, (rho * 2 + e + 1) * 64)
                out[i] = (base[rows] - steep[rows] * pair[i].astype(F32)).astype(BF)


def msa_backward(gain, wc, ws, gb, context, tail, normed, scale, out, bdc, bds):
    spread(wc[...], False, bdc)
    spread(ws[...], False, bds)
    grads = []
    for d in range(2):
        value_grad, gate_grad = [], []
        for h in range(8):
            parts = [gb[h, d, k].astype(F32) for k in range(4)]
            value_grad.append(((parts[0] + parts[1]) + (parts[2] + parts[3])).astype(BF))
            gate_grad.append((tail[h, d] * context[h, d].astype(F32)).astype(BF))
        grad = mm_nt(jnp.concatenate(value_grad, axis=1), bdc[...])
        grad += mm_nt(jnp.concatenate(gate_grad, axis=1), bds[...])
        grads += [grad[:, k * 128 : (k + 1) * 128] for k in range(8)]
    ones = averager()
    scaled = jnp.concatenate(grads, axis=0) * twice(gain)
    xhat = normed[...]
    result = scale[...] * (
        scaled - half_means(scaled, ones) - xhat * half_means(scaled * xhat, ones)
    )
    for k in range(16):
        rows = result[k * 64 : (k + 1) * 64]
        out[2 * k] = rows[:, 0:64].astype(BF)
        out[2 * k + 1] = rows[:, 64:128].astype(BF)


def exchange(x, axes):
    return lax.all_to_all(x, axes, 0, 0, tiled=True)


def swap(x, k):
    return lax.ppermute(x, "b", [(i, i ^ k) for i in range(4)])


def shape(dims, dtype):
    return jax.ShapeDtypeStruct(dims, dtype)


def shards(msa, pair, adj, flags, chains, positions, msa_gain, pair_gain, wc, ws, wf, wp, table):
    vm = pl.BlockSpec()
    sm = pl.BlockSpec(memory_space=pltpu.SMEM)
    gp, rd = ("row", "d", "a"), ("row", "d")
    gain = msa_gain.reshape(1, 64)
    block = lax.axis_index("b").reshape(1)
    piece = shape((8, 2, 64, 128), BF)

    u_send, values, tail = pl.pallas_call(
        msa_forward,
        out_shape=(piece, piece, shape((8, 2, 64, 128), F32)),
        in_specs=[sm] + [vm] * 6,
        out_specs=(vm, vm, vm),
        scratch_shapes=[pltpu.VMEM((1024, 1024), BF)] * 3,
        compiler_params=WHOLE,
        name="msa_forward",
    )(flags, msa, adj, gain, wc, ws, wf)
    mine = exchange(u_send.reshape(16, 64, 128), rd).reshape(8, 2, 64, 128)
    first, third = swap(mine, 1), swap(mine, 3)
    second = swap(first[:4], 3), swap(third[4:], 1)
    ub = pl.pallas_call(
        gather_updates,
        out_shape=shape((8, 512, 128), BF),
        in_specs=[sm] + [vm] * 5,
        out_specs=vm,
        compiler_params=VMEM,
        name="gather_updates",
    )(block, mine, first, *second, third)

    col = lax.axis_index("d") * 16 + lax.axis_index("b") * 4 + lax.axis_index("a")
    def const(*dims):
        return pl.BlockSpec(dims, lambda k: (0,) * len(dims))

    anywhere = pl.BlockSpec(memory_space=pl.ANY)
    vw_send, saved, proj = pl.pallas_call(
        pair_forward,
        grid=(4,),
        out_shape=(shape((8, 2, 4, 112, 128), BF), shape((16, 24, 1024), F32), shape((8, 128), F32)),
        in_specs=[
            sm,
            sm,
            sm,
            sm,
            const(16, 128),
            const(16, 128),
            pl.BlockSpec((64, 64, 128), lambda k: (k, 0, 0)),
            const(1, 128),
            const(8, 128),
            const(8, table.shape[0]),
            const(8, 2, 64, 128),
            anywhere,
        ],
        out_specs=(
            pl.BlockSpec((8, 2, 1, 112, 128), lambda k: (0, 0, k, 0, 0)),
            pl.BlockSpec((4, 24, 1024), lambda k: (k, 0, 0)),
            const(8, 128),
        ),
        scratch_shapes=[pltpu.VMEM((8, 32, 128), F32)] * 2 + [pltpu.VMEM((8, 128), F32)],
        compiler_params=WHOLE,
        name="pair_forward",
    )(
        lax.axis_index("row").reshape(1),
        col.reshape(1),
        chains,
        positions,
        chains.reshape(16, 128),
        positions.reshape(16, 128),
        pair,
        pair_gain.reshape(1, 128),
        wp.T,
        table.T,
        values,
        mine,
    )
    vw_send = pl.pallas_call(
        lambda *refs: None,
        out_shape=shape((8, 2, 4, 112, 128), BF),
        in_specs=[anywhere] * 3,
        out_specs=anywhere,
        input_output_aliases={0: 0},
        compiler_params=WHOLE,
        name="in_order",
    )(vw_send, first, third)
    vw = exchange(vw_send.reshape(64, 112, 128), gp).reshape(8, 8, 112, 128)

    halves = shape((1056, 128), BF)
    p_raw, stats, own, first, third = pl.pallas_call(
        merge_products,
        out_shape=(shape((8, 2, 2, 16, 512), BF), shape((32, 128), BF), shape((2, 8, 2, 64, 128), BF), halves, halves),
        in_specs=[sm, vm, vm],
        out_specs=(vm,) * 5,
        scratch_shapes=[pltpu.VMEM((8, 2, 2, 16, 128), F32), pltpu.VMEM((8, 512, 128), BF)],
        compiler_params=VMEM,
        name="merge_products",
    )(block, ub, vw)
    far, first, third = swap(stats, 2), swap(first, 1), swap(third, 3)
    scores, normed, scale = pl.pallas_call(
        score_products,
        out_shape=(shape((512, 512), F32), shape((1024, 128), F32), shape((1024, 128), F32)),
        in_specs=[vm] * 3,
        out_specs=(vm,) * 3,
        compiler_params=VMEM,
        name="score_products",
    )(msa, ub, vw)
    gd_send = pl.pallas_call(
        gradients,
        out_shape=shape((8, 8, 96, 128), BF),
        in_specs=[vm] * 7,
        out_specs=vm,
        compiler_params=VMEM,
        name="gradients",
    )(stats, first, far, third, p_raw, ub, scores)
    gd = exchange(gd_send.reshape(64, 96, 128), gp).reshape(8, 2, 4, 96, 128)
    half = shape((4, 2, 64, 128), BF)
    to_third, to_first, base = pl.pallas_call(
        context_on_the_way,
        out_shape=(half, half, shape((8, 2, 64, 128), F32)),
        in_specs=[sm] + [vm] * 5,
        out_specs=(vm, vm, vm),
        scratch_shapes=[pltpu.VMEM((512, 8), F32)],
        compiler_params=WHOLE,
        name="context_on_the_way",
    )(block, stats, far, own, first, third)
    context_send = pl.pallas_call(
        context_sum,
        out_shape=piece,
        in_specs=[vm] * 3,
        out_specs=vm,
        compiler_params=WHOLE,
        name="context_sum",
    )(base, swap(to_third, 3), swap(to_first, 1))
    context = exchange(context_send.reshape(16, 64, 128), rd).reshape(8, 2, 64, 128)
    pair_gradient = pl.pallas_call(
        pair_backward,
        grid=(4,),
        out_shape=shape((256, 64, 128), BF),
        in_specs=[
            pl.BlockSpec((64, 64, 128), lambda k: (k, 0, 0)),
            pl.BlockSpec((8, 2, 1, 32, 128), lambda k: (0, 0, k, 2, 0)),
            pl.BlockSpec((4, 24, 1024), lambda k: (k, 0, 0)),
            const(8, 128),
        ],
        out_specs=pl.BlockSpec((64, 64, 128), lambda k: (k, 0, 0)),
        scratch_shapes=[pltpu.VMEM((8, 32, 128), F32)],
        compiler_params=VMEM,
        name="pair_backward",
    )(pair, gd, saved, proj)
    alignment_gradient = pl.pallas_call(
        msa_backward,
        grid=(1,),
        out_shape=shape((32, 64, 64), BF),
        in_specs=[
            const(1, 64),
            const(64, 64),
            const(64, 64),
            const(8, 2, 4, 64, 128),
            const(8, 2, 64, 128),
            const(8, 2, 64, 128),
            const(1024, 128),
            const(1024, 128),
        ],
        out_specs=const(32, 64, 64),
        scratch_shapes=[pltpu.VMEM((1024, 1024), BF)] * 2,
        compiler_params=WHOLE,
        name="msa_backward",
    )(gain, wc, ws, gd, context, tail, normed, scale)
    return (alignment_gradient, pair_gradient)


def solution(mesh):
    inner = Mesh(mesh.devices.reshape(8, 2, 4, 4), ("row", "d", "b", "a"))
    res = ("d", "b", "a")
    split = P("row", res, None)
    return jax.shard_map(
        shards,
        mesh=inner,
        in_specs=(split, split, split, P("row")) + (P(),) * 9,
        out_specs=(split, split),
        check_vma=False,
    )
```

```python
import functools

import jax
import jax.numpy as jnp
from jax import lax
from jax.experimental import pallas as pl
from jax.experimental.pallas import tpu as pltpu
from jax.sharding import Mesh
from jax.sharding import PartitionSpec as P

RMAX = 32
EPS = 1e-05
BF = jnp.bfloat16
F32 = jnp.float32
VMEM = pltpu.CompilerParams(vmem_limit_bytes=48 * 1024 * 1024)
WHOLE = pltpu.CompilerParams(vmem_limit_bytes=60 * 1024 * 1024)
HALF = 64


def mm(a, b):
    return lax.dot_general(a, b, (((1,), (0,)), ((), ())), preferred_element_type=F32)


def mm_nt(a, b):
    return lax.dot_general(a, b, (((1,), (1,)), ((), ())), preferred_element_type=F32)


def mm_tn(a, b):
    return lax.dot_general(a, b, (((0,), (0,)), ((), ())), preferred_element_type=F32)


def iota(shape, dim):
    return lax.broadcasted_iota(jnp.int32, shape, dim)


def split3(x):
    hi = x.astype(BF).astype(F32)
    mid = (x - hi).astype(BF).astype(F32)
    return hi, mid, x - hi - mid


def spread(weight, transposed, out_ref):
    k, l = iota((64, 1024), 0), iota((64, 1024), 1)
    pick = jnp.where((k // 8 == l // 128) & (k % 8 == l % 8), 1.0, 0.0).astype(BF)
    wide = mm_tn(weight, pick) if transposed else mm(weight, pick)
    owner = (l % 128) // 8
    for s in range(16):
        out_ref[s * 64 : (s + 1) * 64, :] = jnp.where(owner == s, wide, 0.0).astype(BF)


def averager():
    half = (iota((128, 128), 0) < 64) == (iota((128, 128), 1) < 64)
    return jnp.where(half, 1.0 / 64, 0.0).astype(BF)


def half_means(x, ones):
    hi = x.astype(BF)
    return mm(hi, ones) + mm((x - hi.astype(F32)).astype(BF), ones)


def paired(x):
    return jnp.concatenate([jnp.concatenate([x(2 * k), x(2 * k + 1)], axis=1) for k in range(16)], axis=0)


def beside(x, d):
    return jnp.concatenate([x[(d * 8 + k) * 64 : (d * 8 + k + 1) * 64] for k in range(8)], axis=1)


def standardize(x, ones):
    center = x.astype(F32) - mm(x, ones)
    scale = lax.rsqrt(half_means(center * center, ones) + EPS)
    return center * scale, scale


def twice(gain):
    return jnp.concatenate([gain[...], gain[...]], axis=1)


def msa_forward(flags, msa, adj, gain, wc, ws, wf, u_out, v_out, t_out, bdc, bds, bdf):
    spread(wc[...], False, bdc)
    spread(ws[...], False, bds)
    spread(wf[...], True, bdf)
    normed, _ = standardize(paired(lambda s: msa[s]), averager())
    normed = (normed * twice(gain)).astype(BF)
    masked = paired(lambda s: (adj[s].astype(F32) * flags[s].astype(F32)).astype(BF))
    for d in range(2):
        x = beside(normed, d)
        values = mm(x, bdc[...]).astype(BF)
        gate = jax.nn.sigmoid(mm(x, bds[...]))
        moved = gate * mm(beside(masked, d), bdf[...])
        update = moved.astype(BF)
        tail = moved * (1.0 - gate)
        for h in range(8):
            cols = slice(h * 128, (h + 1) * 128)
            u_out[h, d] = update[:, cols]
            v_out[h, d] = values[:, cols]
            t_out[h, d] = tail[:, cols]


def partner(x, k, lane):
    return jnp.where(lane & k == 0, pltpu.roll(x, 128 - k, 1), pltpu.roll(x, k, 1))


def pair_forward(
    row, col, chain, position, chains, positions, pair, gain, wp, table, v_in, after,
    out, saved, proj, p_s, m_s, w_s,
):
    w_s[...] = jnp.zeros((8, 128), F32)
    w_s[:, 0 : table.shape[1]] = table[...]
    scaled = wp[...] * gain[...]
    scaled = scaled - jnp.mean(scaled, -1, keepdims=True)
    proj[...] = scaled
    w_hi, w_mid, w_lo = split3(scaled)
    ones8 = jnp.full((8, 128), 1.0 / 128, F32)
    lhs = jnp.concatenate([w_hi, w_mid, w_lo, ones8], axis=0).astype(BF)
    ones8 = ones8.astype(BF)
    mean = jnp.full((128, 128), 1.0 / 128, F32).astype(BF)
    b_lhs = jnp.concatenate(list(split3(w_s[...])) + [jnp.zeros((8, 128), F32)], axis=0).astype(BF)
    lane = iota((8, 128), 1)
    klass = iota((128, 1024), 0)
    left = iota((1, 128), 1) < HALF

    def own_columns(ref):
        both = ref[pl.ds(col[0] // 2, 1), :]
        return jnp.where(left == (col[0] % 2 == 0), both, pltpu.roll(both, 64, 1))

    chain_j, position_j = own_columns(chains), own_columns(positions)
    begin = row[0] * 256 + pl.program_id(0) * 64
    for g in range(4):
        x = jnp.concatenate(
            [pair[e * 32 + g * 8 + rho] for rho in range(8) for e in range(2)], axis=0
        )
        center = x.astype(F32) - mm(x, mean)
        square = center * center
        s_hi = square.astype(BF)
        s_lo = (square - s_hi.astype(F32)).astype(BF)
        var = mm_nt(ones8, s_hi) + mm_nt(ones8, s_lo)
        z = mm_nt(lhs, x)
        scale = lax.rsqrt(var + EPS)
        t = (z[0:8] + z[8:16] + z[16:24]) * scale
        saved[g, 0:8, :] = t
        saved[g, 8:16, :] = scale
        saved[g, 16:24, :] = z[24:32]
        bins = []
        for rho in range(8):
            i = begin + g * 8 + rho
            offset = jnp.where(left, position[i], position[i + 32]) - position_j
            near = jnp.clip(offset + RMAX, 0, 2 * RMAX)
            same = jnp.where(left, chain[i], chain[i + 32]) == chain_j
            bins.append(jnp.where(same, near, 2 * RMAX + 1))
        onehot = jnp.where(klass == jnp.concatenate(bins, axis=1), 1.0, 0.0).astype(BF)
        zb = mm(b_lhs, onehot)
        logits = t + (zb[0:8] + zb[8:16] + zb[16:24])
        for rho in range(8):
            part = logits[:, rho * 128 : (rho + 1) * 128]
            top = part
            for k in (1, 2, 4, 8, 16, 32):
                top = jnp.maximum(top, partner(top, k, lane))
            top = top.astype(BF).astype(F32)
            p_s[:, g * 8 + rho, :] = jnp.exp(part - top)
            m_s[:, g * 8 + rho, :] = top
    quarter = iota((16, 128), 1) // 32
    for h in range(8):
        weights = p_s[h].astype(BF)
        low, high = m_s[h, 0:16, :], m_s[h, 16:32, :]
        packed = jnp.where(
            quarter == 0,
            low,
            jnp.where(
                quarter == 1, pltpu.roll(low, 64, 1), jnp.where(quarter == 2, pltpu.roll(high, 64, 1), high)
            ),
        ).astype(BF)
        for d in range(2):
            out[h, d, 0, 0:64, :] = v_in[h, d]
            out[h, d, 0, 64:96, :] = weights
            out[h, d, 0, 96:112, :] = packed


def rows_at(d, block):
    return pl.ds(pl.multiple_of(d * 256 + block * 64, 64), 64)


def gather_updates(block, mine, first, second_a, second_b, third, out):
    for r in range(8):
        second = second_a.at[r] if r < 4 else second_b.at[r - 4]
        for d in range(2):
            for k, x in enumerate((mine.at[r], first.at[r], second, third.at[r])):
                out[r, rows_at(d, block[0] ^ k), :] = x[d]


def merge_products(block, ub, vw, p_out, stats, own, first, third, m_s, c_s):
    lane = iota((128, 128), 1)
    quarter = lane // 32
    left = lane < HALF
    for half in range(2):
        tops = []
        for c in range(8):
            q = vw[:, c, 96:112, :].astype(F32).reshape(128, 128)
            q64 = pltpu.roll(q, 64, 1)
            if half == 0:
                tops.append(jnp.where(quarter == 0, q, jnp.where(quarter == 3, q64, pltpu.roll(q, 32, 1))))
            else:
                tops.append(jnp.where(quarter == 0, q64, jnp.where(quarter == 3, q, pltpu.roll(q, 96, 1))))
        peak = functools.reduce(jnp.maximum, tops)
        crossed = pltpu.roll(peak, 64, 1)
        m_s[:, 0, half] = jnp.where(left, peak, crossed).reshape(8, 16, 128)
        m_s[:, 1, half] = jnp.where(left, crossed, peak).reshape(8, 16, 128)
        rows = slice(64 + half * 16, 80 + half * 16)
        for cp in range(4):
            one, two = [
                vw[:, c, rows, :].astype(F32).reshape(128, 128) * jnp.exp(tops[c] - peak)
                for c in (2 * cp, 2 * cp + 1)
            ]
            cols = slice(cp * 128, (cp + 1) * 128)
            even = jnp.where(left, one, pltpu.roll(two, 64, 1)).astype(BF)
            odd = jnp.where(left, pltpu.roll(one, 64, 1), two).astype(BF)
            p_out[:, 0, half, :, cols] = even.reshape(8, 16, 128)
            p_out[:, 1, half, :, cols] = odd.reshape(8, 16, 128)
    p = p_out[...].reshape(512, 512)
    total = mm(p, jnp.full((512, 128), 1.0, F32).astype(BF))
    acc = jnp.zeros((512, 128), F32)
    for r in range(0, 8, 2):
        v = jnp.concatenate([vw[r + k, :, 0:64, :].reshape(512, 128) for k in range(2)], axis=1)
        c = mm(p, v)
        for k in range(2):
            part = c[:, k * 128 : (k + 1) * 128]
            acc += ub[r + k].reshape(512, 128).astype(F32) * part
            c_s[r + k] = part.astype(BF)
    score = jnp.sum(acc, axis=1, keepdims=True)
    column = iota((512, 128), 1)
    mixed = m_s[...].reshape(512, 128)
    for at, value in enumerate(split3(total)[:2] + split3(jnp.broadcast_to(score, (512, 128)))):
        mixed = jnp.where(column == at + 1, value, mixed)
    rows = jnp.transpose(mixed)[0:8]
    rows = jnp.concatenate([rows[:, q * 128 : (q + 1) * 128] for q in range(4)], axis=0).astype(BF)
    stats[...] = rows
    first[1024:1056, :] = rows
    third[1024:1056, :] = rows
    for d in range(2):
        for r in range(8):
            zero, one, two, three = [c_s[r, rows_at(d, block[0] ^ k), :] for k in range(4)]
            own[0, r, d] = zero
            at = ((r % 4) * 2 + d) * 64
            out, direct, passed = (first, one, two) if r < 4 else (third, three, two)
            own[1, r, d] = three if r < 4 else one
            out[at : at + 64, :] = direct
            out[512 + at : 576 + at, :] = passed


def score_products(msa, ub, vw, out, normed_out, scale_out):
    acc = jnp.zeros((512, 512), F32)
    for r in range(0, 8, 2):
        u = jnp.concatenate([ub[r + k].reshape(512, 128) for k in range(2)], axis=1)
        v = jnp.concatenate([vw[r + k, :, 0:64, :].reshape(512, 128) for k in range(2)], axis=1)
        acc += mm_nt(u, v)
    out[...] = acc
    normed_out[...], scale_out[...] = standardize(paired(lambda s: msa[s]), averager())


def streamed(stats):
    rows = []
    for ref in stats:
        x = ref[-32:, :].astype(F32)
        rows.append(jnp.concatenate([x[q * 8 : q * 8 + 8] for q in range(4)], axis=1))
    peak = functools.reduce(jnp.maximum, [x[0:1] for x in rows])
    factor = [jnp.exp(x[0:1] - peak) for x in rows]
    total = sum(f * (x[1:2] + x[2:3]) for f, x in zip(factor, rows))
    return [f / total for f in factor], [x[3:4] + x[4:5] + x[5:6] for x in rows]


def gradients(own, first, second, third, p_in, ub, scores, out):
    share, rows = streamed((own, first, second, third))
    row_total = sum(f * x for f, x in zip(share, rows))
    which = iota((8, 512), 0)
    columns = jnp.transpose(jnp.where(which == 0, share[0], jnp.where(which == 1, row_total, 0.0)))
    p = (p_in[...].reshape(512, 512).astype(F32) * columns[:, 0:1]).astype(BF)
    grad = (p.astype(F32) * (scores[...] - columns[:, 1:2])).reshape(8, 2, 32, 512)
    left = iota((256, 128), 1) < HALF
    for cp in range(4):
        cols = slice(cp * 128, (cp + 1) * 128)
        even, odd = [grad[:, e, :, cols].reshape(256, 128) for e in range(2)]
        one = jnp.where(left, even, pltpu.roll(odd, 64, 1)).astype(BF)
        two = jnp.where(left, pltpu.roll(even, 64, 1), odd).astype(BF)
        out[:, 2 * cp, 64:96, :] = one.reshape(8, 32, 128)
        out[:, 2 * cp + 1, 64:96, :] = two.reshape(8, 32, 128)
    pt = jnp.transpose(p)
    for r in range(0, 8, 2):
        u = jnp.concatenate([ub[r + k].reshape(512, 128) for k in range(2)], axis=1)
        grad_v = mm(pt, u).astype(BF)
        for k in range(2):
            out[r + k, :, 0:64, :] = grad_v[:, k * 128 : (k + 1) * 128].reshape(8, 64, 128)


def share_columns(stats, f_s):
    share, _ = streamed(stats)
    which = iota((8, 512), 0)
    mixed = jnp.zeros((8, 512), F32)
    for k in range(4):
        mixed = jnp.where(which == k, share[k], mixed)
    f_s[...] = jnp.transpose(mixed)


def context_on_the_way(block, s0, s2, c, first, third, to_third, to_first, base, f_s):
    share_columns((s0, first, s2, third), f_s)
    for d in range(2):
        f_0, f_1, f_3 = [f_s[rows_at(d, block[0] ^ k), :] for k in (0, 1, 3)]
        for r in range(4):
            at = (r * 2 + d) * 64
            near, far = slice(at, at + 64), slice(512 + at, 576 + at)
            to_third[r, d] = (
                c[1, r, d].astype(F32) * f_3[:, 0:1] + first[far, :].astype(F32) * f_3[:, 1:2]
            ).astype(BF)
            to_first[r, d] = (
                c[1, r + 4, d].astype(F32) * f_1[:, 0:1] + third[far, :].astype(F32) * f_1[:, 3:4]
            ).astype(BF)
            base[r, d] = c[0, r, d].astype(F32) * f_0[:, 0:1] + first[near, :].astype(F32) * f_0[:, 1:2]
            base[r + 4, d] = (
                c[0, r + 4, d].astype(F32) * f_0[:, 0:1] + third[near, :].astype(F32) * f_0[:, 3:4]
            )


def pair_backward(pair, grads, saved, proj, out, g_s):
    w_hi, w_mid, _ = split3(proj[...])
    row = iota((8, 128), 0)
    flag = jnp.where(row < 3, 1.0, 0.0)
    rhs = jnp.concatenate([w_hi, w_hi, w_mid, flag], axis=0).astype(BF)
    rhs_a = jnp.concatenate([flag, jnp.zeros((8, 128), F32)], axis=0).astype(BF)
    g_s[...] = grads[:, 0, 0].astype(F32) + grads[:, 1, 0].astype(F32)
    which = iota((8, 1024), 0)

    def stacked(x):
        hi, mid, low = split3(x)
        return jnp.where(which == 0, hi, jnp.where(which == 1, mid, jnp.where(which == 2, low, 0.0)))

    for g in range(4):
        grad = jnp.concatenate([g_s[:, g * 8 + rho, :] for rho in range(8)], axis=1)
        t, scale, mean = saved[g, 0:8, :], saved[g, 8:16, :], saved[g, 16:24, :]
        slope = jnp.sum(grad * t, axis=0, keepdims=True) * (1.0 / 128)
        alpha = scale * scale * slope
        scaled = grad * scale
        hi = scaled.astype(BF).astype(F32)
        lhs = jnp.concatenate([hi, scaled - hi, hi, stacked(alpha * mean)], axis=0).astype(BF)
        lhs_a = jnp.concatenate([stacked(alpha), jnp.zeros((8, 1024), F32)], axis=0).astype(BF)
        base = mm_tn(lhs, rhs)
        steep = mm_tn(lhs_a, rhs_a)
        for rho in range(8):
            for e in range(2):
                i = e * 32 + g * 8 + rho
                rows = slice((rho * 2 + e) * 64, (rho * 2 + e + 1) * 64)
                out[i] = (base[rows] - steep[rows] * pair[i].astype(F32)).astype(BF)


def msa_backward(gain, wc, ws, gb, context, tail, normed, scale, out, bdc, bds):
    spread(wc[...], False, bdc)
    spread(ws[...], False, bds)
    grads = []
    for d in range(2):
        value_grad, gate_grad = [], []
        for h in range(8):
            parts = [gb[h, d, k].astype(F32) for k in range(4)]
            value_grad.append(((parts[0] + parts[1]) + (parts[2] + parts[3])).astype(BF))
            gate_grad.append((tail[h, d] * context[h, d].astype(F32)).astype(BF))
        grad = mm_nt(jnp.concatenate(value_grad, axis=1), bdc[...])
        grad += mm_nt(jnp.concatenate(gate_grad, axis=1), bds[...])
        grads += [grad[:, k * 128 : (k + 1) * 128] for k in range(8)]
    ones = averager()
    scaled = jnp.concatenate(grads, axis=0) * twice(gain)
    xhat = normed[...]
    result = scale[...] * (
        scaled - half_means(scaled, ones) - xhat * half_means(scaled * xhat, ones)
    )
    for k in range(16):
        rows = result[k * 64 : (k + 1) * 64]
        out[2 * k] = rows[:, 0:64].astype(BF)
        out[2 * k + 1] = rows[:, 64:128].astype(BF)


def exchange(x, axes):
    return lax.all_to_all(x, axes, 0, 0, tiled=True)


def swap(x, k):
    return lax.ppermute(x, "b", [(i, i ^ k) for i in range(4)])


def shape(dims, dtype):
    return jax.ShapeDtypeStruct(dims, dtype)


def shards(msa, pair, adj, flags, chains, positions, msa_gain, pair_gain, wc, ws, wf, wp, table):
    vm = pl.BlockSpec()
    sm = pl.BlockSpec(memory_space=pltpu.SMEM)
    gp, rd = ("row", "d", "a"), ("row", "d")
    gain = msa_gain.reshape(1, 64)
    block = lax.axis_index("b").reshape(1)
    piece = shape((8, 2, 64, 128), BF)

    u_send, values, tail = pl.pallas_call(
        msa_forward,
        out_shape=(piece, piece, shape((8, 2, 64, 128), F32)),
        in_specs=[sm] + [vm] * 6,
        out_specs=(vm, vm, vm),
        scratch_shapes=[pltpu.VMEM((1024, 1024), BF)] * 3,
        compiler_params=WHOLE,
        name="msa_forward",
    )(flags, msa, adj, gain, wc, ws, wf)
    mine = exchange(u_send.reshape(16, 64, 128), rd).reshape(8, 2, 64, 128)
    first, third = swap(mine, 1), swap(mine, 3)
    second = swap(first[:4], 3), swap(third[4:], 1)
    ub = pl.pallas_call(
        gather_updates,
        out_shape=shape((8, 512, 128), BF),
        in_specs=[sm] + [vm] * 5,
        out_specs=vm,
        compiler_params=VMEM,
        name="gather_updates",
    )(block, mine, first, *second, third)

    col = lax.axis_index("d") * 16 + lax.axis_index("b") * 4 + lax.axis_index("a")
    def const(*dims):
        return pl.BlockSpec(dims, lambda k: (0,) * len(dims))

    anywhere = pl.BlockSpec(memory_space=pl.ANY)
    vw_send, saved, proj = pl.pallas_call(
        pair_forward,
        grid=(4,),
        out_shape=(shape((8, 2, 4, 112, 128), BF), shape((16, 24, 1024), F32), shape((8, 128), F32)),
        in_specs=[
            sm,
            sm,
            sm,
            sm,
            const(16, 128),
            const(16, 128),
            pl.BlockSpec((64, 64, 128), lambda k: (k, 0, 0)),
            const(1, 128),
            const(8, 128),
            const(8, table.shape[0]),
            const(8, 2, 64, 128),
            anywhere,
        ],
        out_specs=(
            pl.BlockSpec((8, 2, 1, 112, 128), lambda k: (0, 0, k, 0, 0)),
            pl.BlockSpec((4, 24, 1024), lambda k: (k, 0, 0)),
            const(8, 128),
        ),
        scratch_shapes=[pltpu.VMEM((8, 32, 128), F32)] * 2 + [pltpu.VMEM((8, 128), F32)],
        compiler_params=WHOLE,
        name="pair_forward",
    )(
        lax.axis_index("row").reshape(1),
        col.reshape(1),
        chains,
        positions,
        chains.reshape(16, 128),
        positions.reshape(16, 128),
        pair,
        pair_gain.reshape(1, 128),
        wp.T,
        table.T,
        values,
        mine,
    )
    vw_send = pl.pallas_call(
        lambda *refs: None,
        out_shape=shape((8, 2, 4, 112, 128), BF),
        in_specs=[anywhere] * 3,
        out_specs=anywhere,
        input_output_aliases={0: 0},
        compiler_params=WHOLE,
        name="in_order",
    )(vw_send, first, third)
    vw = exchange(vw_send.reshape(64, 112, 128), gp).reshape(8, 8, 112, 128)

    halves = shape((1056, 128), BF)
    p_raw, stats, own, first, third = pl.pallas_call(
        merge_products,
        out_shape=(shape((8, 2, 2, 16, 512), BF), shape((32, 128), BF), shape((2, 8, 2, 64, 128), BF), halves, halves),
        in_specs=[sm, vm, vm],
        out_specs=(vm,) * 5,
        scratch_shapes=[pltpu.VMEM((8, 2, 2, 16, 128), F32), pltpu.VMEM((8, 512, 128), BF)],
        compiler_params=VMEM,
        name="merge_products",
    )(block, ub, vw)
    far, first, third = swap(stats, 2), swap(first, 1), swap(third, 3)
    scores, normed, scale = pl.pallas_call(
        score_products,
        out_shape=(shape((512, 512), F32), shape((1024, 128), F32), shape((1024, 128), F32)),
        in_specs=[vm] * 3,
        out_specs=(vm,) * 3,
        compiler_params=VMEM,
        name="score_products",
    )(msa, ub, vw)
    gd_send = pl.pallas_call(
        gradients,
        out_shape=shape((8, 8, 96, 128), BF),
        in_specs=[vm] * 7,
        out_specs=vm,
        compiler_params=VMEM,
        name="gradients",
    )(stats, first, far, third, p_raw, ub, scores)
    gd = exchange(gd_send.reshape(64, 96, 128), gp).reshape(8, 2, 4, 96, 128)
    half = shape((4, 2, 64, 128), BF)
    to_third, to_first, base = pl.pallas_call(
        context_on_the_way,
        out_shape=(half, half, shape((8, 2, 64, 128), F32)),
        in_specs=[sm] + [vm] * 5,
        out_specs=(vm, vm, vm),
        scratch_shapes=[pltpu.VMEM((512, 8), F32)],
        compiler_params=WHOLE,
        name="context_on_the_way",
    )(block, stats, far, own, first, third)
    far = jnp.concatenate([swap(to_third, 3), swap(to_first, 1)], axis=0)
    context_send = (base + far.astype(F32)).astype(BF)
    context = exchange(context_send.reshape(16, 64, 128), rd).reshape(8, 2, 64, 128)
    pair_gradient = pl.pallas_call(
        pair_backward,
        grid=(4,),
        out_shape=shape((256, 64, 128), BF),
        in_specs=[
            pl.BlockSpec((64, 64, 128), lambda k: (k, 0, 0)),
            pl.BlockSpec((8, 2, 1, 32, 128), lambda k: (0, 0, k, 2, 0)),
            pl.BlockSpec((4, 24, 1024), lambda k: (k, 0, 0)),
            const(8, 128),
        ],
        out_specs=pl.BlockSpec((64, 64, 128), lambda k: (k, 0, 0)),
        scratch_shapes=[pltpu.VMEM((8, 32, 128), F32)],
        compiler_params=VMEM,
        name="pair_backward",
    )(pair, gd, saved, proj)
    alignment_gradient = pl.pallas_call(
        msa_backward,
        grid=(1,),
        out_shape=shape((32, 64, 64), BF),
        in_specs=[
            const(1, 64),
            const(64, 64),
            const(64, 64),
            const(8, 2, 4, 64, 128),
            const(8, 2, 64, 128),
            const(8, 2, 64, 128),
            const(1024, 128),
            const(1024, 128),
        ],
        out_specs=const(32, 64, 64),
        scratch_shapes=[pltpu.VMEM((1024, 1024), BF)] * 2,
        compiler_params=WHOLE,
        name="msa_backward",
    )(gain, wc, ws, gd, context, tail, normed, scale)
    return (alignment_gradient, pair_gradient)


def solution(mesh):
    inner = Mesh(mesh.devices.reshape(8, 2, 4, 4), ("row", "d", "b", "a"))
    res = ("d", "b", "a")
    split = P("row", res, None)
    return jax.shard_map(
        shards,
        mesh=inner,
        in_specs=(split, split, split, P("row")) + (P(),) * 9,
        out_specs=(split, split),
        check_vma=False,
    )
```
